128 devices in a mesh: row: 16 (over x, z), col: 8 (over y, core).
Axes of the slice: x: 4, y: 4, z: 4, core: 2. Of those that a mesh axis runs over, the one named last changes fastest.
Arguments:
- x_tiles: float32 [16, 8, 12, 128, 128], P('row', 'col'), as said below
- block_rows: int32 [16, 8, 12], P('row', 'col'), may hold values from 0 to 48, as said below
- block_cols: int32 [16, 8, 12], P('row', 'col'), may hold values from 0 to 48, as said below
- pair_left: int32 [16, 8, 276], P('row', 'col'), may hold values from 0 to 95, as said below
- pair_right: int32 [16, 8, 276], P('row', 'col'), may hold values from 0 to 191, as said below
- pair_target: int32 [16, 8, 276], P('row', 'col'), may hold values from 0 to 12, as said below
- branches: int32 [4], replicated, may hold values from 0 to 1, as said below
Outputs:
- purified: float32 [16, 8, 12, 128, 128], P('row', 'col')
- traces: float32 [4, 2], replicated
The draws below stay inside these ranges and needn't reach their ends.
Inputs may be any that keep to these rules, and one draw needn't show every extreme that they name: `x_tiles`: X is symmetric and zero outside its stored pattern; a slot that holds no block is zero. The stored pattern is symmetric and holds every diagonal block; every block-row stores the same number of blocks; the block-rows of a device are 3 labels that form its row strip, shared by the devices of that strip; a device stores each position once; a slot that holds no block has block_rows = block_cols = 48; some device uses all 12 slots. `block_cols`: the block-columns of a device are 6 labels that form its column strip, shared by the devices of that strip; 48 marks a slot that holds no block. `pair_left`: for each stored block (i, j) of a device, its list holds exactly one entry for every k with (i, k) and (k, j) both stored, and no other used entry. Unused entries hold 0. `pair_right`: unused entries hold 0. `pair_target`: used entries come first on each device; a target of 12 marks an unused entry; on some device all 276 entries are used. Both branches occur among the steps.
All inputs are finite; a program needn't handle non-finite values.
Results may differ from the reference program's by a relative error of at most 0.0003.
Values sent between devices are 32-bit elements; how exact they have to be, the bound alone decides.
A program may use at most 192 MiB of HBM per device.

```python
import jax
import jax.numpy as jnp
from jax import lax

BLK = 128
BR = 3
STEPS = 4
SLOTS = 12
PAIRS = 276
NB = 48
N_ROW = 16
N_COL = 8


def layout(key):
    key = jax.random.fold_in(key, 7)
    key_label, key_slot = jax.random.split(key, 2)
    nb_all = BR * N_ROW
    reach = 2 * N_COL - 1
    slot_count = 4 * BR
    devices = N_ROW * N_COL
    device = jnp.arange(devices, dtype=jnp.int32)
    dev_row = device // N_COL
    dev_col = device % N_COL
    residue = (dev_col - dev_row) % N_COL
    canon = jnp.arange(slot_count, dtype=jnp.int32)
    offset = residue[:, None] + N_COL * (canon[None, :] % 4 - 2)
    live = jnp.abs(offset) <= reach
    phys_row = dev_row[:, None] + N_ROW * (canon[None, :] // 4)
    phys_col = (phys_row + offset) % nb_all
    slot_keys = jax.random.split(key_slot, devices)
    order = jax.vmap(lambda one_key: jax.random.permutation(one_key, slot_count))(slot_keys).astype(jnp.int32)
    position = jnp.argsort(order, axis=-1).astype(jnp.int32)
    labels = jax.random.permutation(key_label, nb_all).astype(jnp.int32)
    return (dev_row, dev_col, offset, live, phys_row, phys_col, order, position, labels)


def stored_pattern(key):
    dev_row, dev_col, offset, live, phys_row, phys_col, order, position, labels = layout(key)
    nb_all = BR * N_ROW
    live_at = jnp.take_along_axis(live, order, axis=-1)
    rows_at = jnp.take_along_axis(phys_row, order, axis=-1)
    cols_at = jnp.take_along_axis(phys_col, order, axis=-1)
    label_rows = jnp.where(live_at, labels[rows_at], nb_all).astype(jnp.int32)
    label_cols = jnp.where(live_at, labels[cols_at], nb_all).astype(jnp.int32)
    return (label_rows, label_cols, live_at, rows_at, cols_at)


def product_list(key):
    dev_row, dev_col, offset, live, phys_row, phys_col, order, position, labels = layout(key)
    key = jax.random.fold_in(key, 11)
    nb_all = BR * N_ROW
    reach = 2 * N_COL - 1
    slot_count = 4 * BR
    devices = N_ROW * N_COL
    steps_a = jnp.arange(-reach, reach + 1, dtype=jnp.int32)
    remain = offset[:, :, None] - steps_a[None, None, :]
    valid = live[:, :, None] & (jnp.abs(remain) <= reach)
    row_turn = (jnp.arange(slot_count, dtype=jnp.int32) // 4)[None, :, None]
    left_col = (dev_row[:, None, None] + steps_a[None, None, :]) % N_COL
    left_m = (steps_a - steps_a % N_COL) // N_COL + 2
    left_canon = row_turn * 4 + left_m[None, None, :]
    left_device = dev_row[:, None, None] * N_COL + left_col
    left_index = left_col * slot_count + position[left_device, left_canon]
    inner = (phys_row[:, :, None] + steps_a[None, None, :]) % nb_all
    right_row = inner % N_ROW
    right_turn = inner // N_ROW
    remain_safe = jnp.clip(remain, -reach, reach)
    right_m = (remain_safe - remain_safe % N_COL) // N_COL + 2
    right_device = right_row * N_COL + dev_col[:, None, None]
    right_index = right_row * slot_count + position[right_device, right_turn * 4 + right_m]
    target_index = jnp.broadcast_to(position[:, :, None], remain.shape)
    count = slot_count * steps_a.shape[0]
    flat_valid = valid.reshape(devices, count)
    rank_keys = jax.random.split(key, devices)
    ranks = jax.vmap(lambda one_key: jax.random.permutation(one_key, count))(rank_keys).astype(jnp.int32)
    scores = jnp.where(flat_valid, 0, count).astype(jnp.int32) + ranks
    chosen = jnp.argsort(scores, axis=-1)[:, :PAIRS]
    used = jnp.take_along_axis(flat_valid, chosen, axis=-1)
    left_ids = jnp.where(used, jnp.take_along_axis(left_index.reshape(devices, count), chosen, axis=-1), 0)
    right_ids = jnp.where(used, jnp.take_along_axis(right_index.reshape(devices, count), chosen, axis=-1), 0)
    target_ids = jnp.where(used, jnp.take_along_axis(target_index.reshape(devices, count), chosen, axis=-1), slot_count)
    shape = (N_ROW, N_COL, PAIRS)
    return (left_ids.reshape(shape).astype(jnp.int32), right_ids.reshape(shape).astype(jnp.int32), target_ids.reshape(shape).astype(jnp.int32))


def draw_block_rows(key, part):
    return stored_pattern(key)[0].reshape(N_ROW, N_COL, SLOTS)


def draw_block_cols(key, part):
    return stored_pattern(key)[1].reshape(N_ROW, N_COL, SLOTS)


def draw_pair_left(key, part):
    return product_list(key)[0]


def draw_pair_right(key, part):
    return product_list(key)[1]


def draw_pair_target(key, part):
    return product_list(key)[2]


def draw_branches(key, part):
    key = jax.random.fold_in(key, 5)
    picked = jax.random.randint(key, (STEPS,), 0, 2).astype(jnp.int32)
    index = jnp.arange(STEPS, dtype=jnp.int32)
    return jnp.where(index == 1, 1 - picked[0], picked).astype(jnp.int32)


def draw_x_tiles(key, part):
    label_rows, label_cols, live_at, rows_at, cols_at = stored_pattern(key)
    key = jax.random.fold_in(key, 3)
    key_values, key_diag = jax.random.split(key, 2)
    nb_all = BR * N_ROW
    reach = 2 * N_COL - 1
    spread = 0.25 * (BLK * (2 * reach + 1)) ** (-0.5)
    identity = (jnp.arange(BLK)[:, None] == jnp.arange(BLK)[None, :]).astype(jnp.float32)

    def one_block(row_at, col_at):
        lower = jnp.minimum(row_at, col_at)
        upper = jnp.maximum(row_at, col_at)
        block_key = jax.random.fold_in(key_values, lower * nb_all + upper)
        raw = jax.random.normal(block_key, (BLK, BLK), jnp.float32)
        raw = jnp.where(row_at > col_at, raw.T, raw)
        raw = jnp.where(row_at == col_at, (raw + raw.T) * 0.70710678, raw)
        ramp = 1.0 + 2.0 * (row_at % N_ROW).astype(jnp.float32) / (N_ROW - 1)
        amount = jax.random.uniform(jax.random.fold_in(key_diag, row_at), (BLK,), jnp.float32, 0.15, 0.35) * ramp
        on_diagonal = jnp.where(row_at == col_at, 1.0, 0.0).astype(jnp.float32)
        return raw * spread + on_diagonal * identity * amount[None, :]
    blocks = jax.vmap(one_block)(rows_at.reshape(-1), cols_at.reshape(-1))
    blocks = blocks * live_at.reshape(-1).astype(jnp.float32)[:, None, None]
    return blocks.reshape(N_ROW, N_COL, SLOTS, BLK, BLK).astype(jnp.float32)


def setup_inputs(seed: int = 0) -> dict:
    streams_of = jax.random.split(jax.random.key(seed), 8)
    return {
        "x_tiles": draw_x_tiles(jax.random.fold_in(streams_of[7], 71), 0),
        "block_rows": draw_block_rows(jax.random.fold_in(streams_of[7], 71), 0),
        "block_cols": draw_block_cols(jax.random.fold_in(streams_of[7], 71), 0),
        "pair_left": draw_pair_left(jax.random.fold_in(streams_of[7], 71), 0),
        "pair_right": draw_pair_right(jax.random.fold_in(streams_of[7], 71), 0),
        "pair_target": draw_pair_target(jax.random.fold_in(streams_of[7], 71), 0),
        "branches": draw_branches(jax.random.fold_in(streams_of[7], 71), 0),
    }


def slot_products(strip_left, strip_right, left_ids, right_ids, target_ids):
    left_blocks = jnp.take(strip_left, left_ids, axis=0)
    right_blocks = jnp.take(strip_right, right_ids, axis=0)
    block_product = jnp.einsum('pij,pjk->pik', left_blocks, right_blocks, precision=lax.Precision.HIGHEST)
    weights = (target_ids[:, None] == jnp.arange(SLOTS, dtype=jnp.int32)[None, :]).astype(jnp.float32)
    return jnp.einsum('ps,pik->sik', weights, block_product, precision=lax.Precision.HIGHEST)


def diagonal_sum(stored, is_diagonal):
    sums = jnp.sum(jnp.diagonal(stored, axis1=-2, axis2=-1), axis=-1)
    return jnp.sum(jnp.where(is_diagonal, sums, jnp.zeros_like(sums)))


def reference(x_tiles, block_rows, block_cols, pair_left, pair_right, pair_target, branches):
    is_diagonal = (block_rows == block_cols) & (block_rows < NB)
    scale = 1.0 / (NB * BLK)
    purified = x_tiles
    found_traces = []
    for step_index in range(STEPS):
        def per_device(flat_index):
            row_at = flat_index // N_COL
            col_at = flat_index % N_COL
            strip_left = purified[row_at].reshape(N_COL * SLOTS, BLK, BLK)
            strip_right = purified[:, col_at].reshape(N_ROW * SLOTS, BLK, BLK)
            return slot_products(strip_left, strip_right, pair_left[row_at, col_at], pair_right[row_at, col_at], pair_target[row_at, col_at])

        squared = lax.map(per_device, jnp.arange(N_ROW * N_COL, dtype=jnp.int32)).reshape(N_ROW, N_COL, SLOTS, BLK, BLK)
        trace_now = diagonal_sum(purified, is_diagonal)
        trace_square = diagonal_sum(squared, is_diagonal)
        found_traces.append(jnp.stack([trace_now, trace_square]))
        purified = jnp.where(branches[step_index] == 1, squared, 2.0 * purified - squared)
    return purified, jnp.stack(found_traces) * scale
```

```python
import jax
import jax.numpy as jnp
from jax import lax
from jax.experimental import pallas as pl
from jax.experimental.pallas import tpu as pltpu
from jax.sharding import PartitionSpec as P

MESH = pl.DeviceIdType.MESH
BR = 3
STEPS = 4
BLK = 128
SLOTS = 12
ROWS = 16
COLS = 8
DEPTH = 32
CHUNKS = 4
CS = SLOTS // CHUNKS
GROUP = 8


def zbits(z):
    low = ((z + 1) // 2) % 2
    high = z // 2
    return low, high


def kernel(table, coef, x_hbm, out_hbm, tr, xs, lf, rf, ls, rs, acc, r_l, r_r, s_l, s_r, sw_s, sw_r, fin_s, fin_r, credit):
    row = lax.axis_index("row")
    col = lax.axis_index("col")
    x, z, y, p = row // 4, row % 4, col // 2, col % 2
    low, high = zbits(z)
    moved = p != low

    z_low = z + 1 - 2 * (z % 2)
    z_high = 3 - z
    partner = (x * 4 + z_low, y * 2 + 1 - p)
    sibling = (row, y * 2 + 1 - p)
    l_next = (row, ((y + 1) % 4) * 2 + p)
    l_prev = (row, ((y + 3) % 4) * 2 + p)
    l_pair = (x * 4 + z_low, col)
    r_next = (((x + 1) % 4) * 4 + z, col)
    r_prev = (((x + 3) % 4) * 4 + z, col)
    r_pair = (x * 4 + z_high, col)
    neighbours = (l_next, l_prev, l_pair, r_next, r_prev, r_pair, sibling)

    barrier = pltpu.get_barrier_semaphore()
    for device in neighbours + (partner,):
        pl.semaphore_signal(barrier, inc=1, device_id=device, device_id_type=MESH)
    pl.semaphore_wait(barrier, len(neighbours) + 1)

    def roles(q, h, unit):
        a, b, c = (q + 3) % 4, (q + 1) % 4, (q + 2) % 4
        g = 1 - h
        return [unit(q, h), unit(a, h), unit(b, h), unit(q, g), unit(c, h), unit(a, g), unit(b, g), unit(c, g)]

    units_l = roles(y, low, lambda q, h: q * 2 + h)
    units_r = roles(x, high, lambda q, h: q * 4 + h * 3 + p * (1 - 2 * h))
    units_s = roles(x, high, lambda q, h: q * 4 + h * 3 + (1 - p) * (1 - 2 * h))

    def part(m):
        return pl.ds(m * CS, CS)

    def copy(src, dst, ssem, rsem, device):
        return pltpu.make_async_remote_copy(
            src_ref=src, dst_ref=dst, send_sem=ssem, recv_sem=rsem, device_id=device, device_id_type=MESH
        )

    class Gather:
        def __init__(self, buf, units, rsem, ssem, nxt, prv, pair):
            self.buf, self.units, self.rsem, self.ssem = buf, units, rsem, ssem
            self.nxt, self.prv, self.pair = nxt, prv, pair

        def source(self, role, m):
            return xs.at[part(m)] if role == 0 else self.buf.at[self.units[role], part(m)]

        def plan(self, m):
            nxt, prv, pair = self.nxt, self.prv, self.pair
            first = [(0, nxt, 1), (0, prv, 2), (0, pair, 3)]
            second = [(1, nxt, 4)] if m % 2 == 0 else [(2, prv, 4)]
            if m < CHUNKS // 2:
                second += [(1, pair, 5), (2, pair, 6)]
                third = [(4, pair, 7)]
            else:
                second += [(3, nxt, 5), (3, prv, 6)]
                third = [(5, nxt, 7)] if m % 2 == 0 else [(6, prv, 7)]
            return first, second, third

        def sends(self, m, level):
            plan = self.plan(m)
            at = sum(len(one) for one in plan[:level])
            made = []
            for index, (role, device, there) in enumerate(plan[level]):
                made.append(
                    copy(
                        self.source(role, m),
                        self.buf.at[self.units[role], part(m)],
                        self.ssem.at[m, at + index],
                        self.rsem.at[m, there - 1],
                        device,
                    )
                )
            return made

        def arrived(self, m, role):
            place = self.buf.at[self.units[role], part(m)]
            copy(place, place, self.ssem.at[m, 0], self.rsem.at[m, role - 1], self.nxt).wait_recv()

    left = Gather(lf, units_l, r_l, s_l, l_next, l_prev, l_pair)
    right = Gather(rf, units_r, r_r, s_r, r_next, r_prev, r_pair)

    def share(m, role):
        place = rf.at[units_r[role], part(m)]
        return copy(right.source(role, m), place, s_r.at[m, 7 + role], r_r.at[m, 7 + role], sibling)

    def shared(m, role):
        place = rf.at[units_s[role], part(m)]
        copy(place, place, s_r.at[m, 0], r_r.at[m, 7 + role], sibling).wait_recv()

    def send_own(m):
        for one in left.sends(m, 0) + right.sends(m, 0) + [share(m, 0)]:
            one.start()

    def split(value):
        top = value.astype(jnp.bfloat16)
        return top, (value - top.astype(jnp.float32)).astype(jnp.bfloat16)

    def keep_left(unit, block, value):
        top, low_part = split(value)
        ls[unit * SLOTS + block, 0:BLK] = top
        ls[unit * SLOTS + block, BLK : 2 * BLK] = low_part

    def keep_right(unit, block, value):
        top, low_part = split(value)
        rs[unit * SLOTS + block, :, 0:BLK] = top
        rs[unit * SLOTS + block, :, BLK : 2 * BLK] = low_part

    def prepare_left(m, role):
        unit = units_l[role]

        @pl.loop(m * CS, (m + 1) * CS)
        def _(block):
            keep_left(unit, block, lf[unit, block])

    def prepare_right(m, unit):
        @pl.loop(m * CS, (m + 1) * CS)
        def _(block):
            keep_right(unit, block, rf[unit, block])

    def gather(step):
        def level(m, number, waits):
            for role in waits:
                left.arrived(m, role)
                right.arrived(m, role)
            for one in left.sends(m, number) + right.sends(m, number) + [share(m, role) for role in waits]:
                one.start()

        def prepare(m, waits):
            for role in waits:
                prepare_left(m, role)
                prepare_right(m, units_r[role])

        for m in range(CHUNKS):
            level(m, 1, (1, 2, 3))

        @pl.loop(0, SLOTS)
        def _(block):
            value = xs[block]
            keep_left(units_l[0], block, value)
            keep_right(units_r[0], block, value)

        for m in range(CHUNKS):
            prepare(m, (1, 2, 3))
            shared(m, 0)
            prepare_right(m, units_s[0])
        for m in range(CHUNKS):
            level(m, 2, (4, 5, 6))
            for role in (1, 2, 3):
                shared(m, role)
                prepare_right(m, units_s[role])
        for m in range(CHUNKS):
            prepare(m, (4, 5, 6))
            left.arrived(m, 7)
            right.arrived(m, 7)
            share(m, 7).start()
            prepare(m, (7,))
            for role in (4, 5, 6):
                shared(m, role)
                prepare_right(m, units_s[role])
        for m in range(CHUNKS):
            shared(m, 7)
            prepare_right(m, units_s[7])
            for number in range(3):
                for one in left.sends(m, number) + right.sends(m, number):
                    one.wait_send()
            for role in range(8):
                share(m, role).wait_send()

            @pl.when(step < STEPS - 1)
            def _():
                for device in neighbours:
                    pl.semaphore_signal(credit.at[m], inc=1, device_id=device, device_id_type=MESH)

    diagonal = lax.broadcasted_iota(jnp.int32, (BLK, BLK), 0) == lax.broadcasted_iota(jnp.int32, (BLK, BLK), 1)

    def trace_terms(value, weight):
        kept = jnp.where(diagonal, value, 0.0)
        return jnp.sum(kept.reshape(BLK // 8, 8, BLK), axis=0) * weight

    def multiply(step, m):
        @pl.loop(m * CS, (m + 1) * CS)
        def _(target):
            acc[...] = jnp.zeros_like(acc)

            @pl.loop(0, DEPTH // GROUP)
            def _(turn):
                first = turn * GROUP
                lhs = jnp.concatenate([ls[table[target, first + i]] for i in range(GROUP)], axis=1)
                rhs = jnp.concatenate([rs[table[target, DEPTH + first + i]] for i in range(GROUP)], axis=0)
                acc[...] += jnp.dot(lhs, rhs, preferred_element_type=jnp.float32)

            squared = acc[0:BLK, 0:BLK] + (
                acc[0:BLK, BLK : 2 * BLK] + acc[BLK : 2 * BLK, 0:BLK] + acc[BLK : 2 * BLK, BLK : 2 * BLK]
            )
            stored = xs[target]
            weight = table[SLOTS, target].astype(jnp.float32)
            tr[2 * step] += trace_terms(stored, weight)
            tr[2 * step + 1] += trace_terms(squared, weight)
            xs[target] = coef[step, 0] * stored + coef[step, 1] * squared

    for m in range(CHUNKS):
        remote = copy(x_hbm.at[part(m)], xs.at[part(m)], sw_s.at[m], sw_r.at[m], partner)
        local = pltpu.make_async_copy(x_hbm.at[part(m)], xs.at[part(m)], sw_r.at[m])
        pl.when(moved)(remote.start)
        pl.when(jnp.logical_not(moved))(local.start)
    tr[...] = jnp.zeros_like(tr)
    ls[COLS * SLOTS] = jnp.zeros((2 * BLK, BLK), jnp.bfloat16)
    for m in range(CHUNKS):
        remote = copy(x_hbm.at[part(m)], xs.at[part(m)], sw_s.at[m], sw_r.at[m], partner)
        local = pltpu.make_async_copy(x_hbm.at[part(m)], xs.at[part(m)], sw_r.at[m])
        pl.when(moved)(remote.wait)
        pl.when(jnp.logical_not(moved))(local.wait)
        send_own(m)

    def finals(m):
        remote = copy(xs.at[part(m)], out_hbm.at[part(m)], fin_s.at[m], fin_r.at[m], partner)
        local = pltpu.make_async_copy(xs.at[part(m)], out_hbm.at[part(m)], fin_r.at[m])
        return remote, local

    @pl.loop(0, STEPS)
    def _(step):
        gather(step)
        for m in range(CHUNKS):
            multiply(step, m)

            @pl.when(step < STEPS - 1)
            def _():
                pl.semaphore_wait(credit.at[m], len(neighbours))
                send_own(m)

            @pl.when(step == STEPS - 1)
            def _():
                remote, local = finals(m)
                pl.when(moved)(remote.start)
                pl.when(jnp.logical_not(moved))(local.start)

    for m in range(CHUNKS):
        remote, local = finals(m)
        pl.when(moved)(remote.wait)
        pl.when(jnp.logical_not(moved))(local.wait)


def run(table, coef, blocks):
    dma = pltpu.SemaphoreType.DMA
    anywhere = pl.BlockSpec(memory_space=pl.ANY)
    scalars = pl.BlockSpec(memory_space=pltpu.SMEM)
    return pl.pallas_call(
        kernel,
        out_shape=(
            jax.ShapeDtypeStruct((SLOTS, BLK, BLK), jnp.float32),
            jax.ShapeDtypeStruct((2 * STEPS, 8, BLK), jnp.float32),
        ),
        in_specs=[scalars, scalars, anywhere],
        out_specs=(anywhere, pl.BlockSpec(memory_space=pltpu.VMEM)),
        scratch_shapes=[
            pltpu.VMEM((SLOTS, BLK, BLK), jnp.float32),
            pltpu.VMEM((COLS, SLOTS, BLK, BLK), jnp.float32),
            pltpu.VMEM((ROWS, SLOTS, BLK, BLK), jnp.float32),
            pltpu.VMEM((COLS * SLOTS + 1, 2 * BLK, BLK), jnp.bfloat16),
            pltpu.VMEM((ROWS * SLOTS, BLK, 2 * BLK), jnp.bfloat16),
            pltpu.VMEM((2 * BLK, 2 * BLK), jnp.float32),
            dma((CHUNKS, 7)),
            dma((CHUNKS, 15)),
            dma((CHUNKS, 7)),
            dma((CHUNKS, 15)),
            dma((CHUNKS,)),
            dma((CHUNKS,)),
            dma((CHUNKS,)),
            dma((CHUNKS,)),
            pltpu.SemaphoreType.REGULAR((CHUNKS,)),
        ],
        compiler_params=pltpu.CompilerParams(
            collective_id=0, has_side_effects=True, vmem_limit_bytes=52 * 2**20
        ),
        cost_estimate=pl.CostEstimate(
            flops=STEPS * SLOTS * DEPTH * 8 * BLK**3, bytes_accessed=2 * SLOTS * BLK * BLK * 4, transcendentals=0
        ),
    )(table, coef, blocks)


def product_table(left_ids, right_ids, target_ids):
    count = target_ids.shape[0]
    order = jnp.arange(count, dtype=jnp.int32)
    same = (target_ids[:, None] == target_ids[None, :]) & (order[None, :] < order[:, None])
    place = target_ids * DEPTH + jnp.sum(same.astype(jnp.int32), axis=1)
    chosen = place[:, None] == jnp.arange(SLOTS * DEPTH, dtype=jnp.int32)[None, :]
    lefts = jnp.sum(jnp.where(chosen, left_ids[:, None] - COLS * SLOTS, 0), axis=0) + COLS * SLOTS
    rights = jnp.sum(jnp.where(chosen, right_ids[:, None], 0), axis=0)
    return jnp.concatenate([lefts.reshape(SLOTS, DEPTH), rights.reshape(SLOTS, DEPTH)], axis=1)


def partners():
    pairs = []
    for row in range(ROWS):
        for col in range(COLS):
            z, p = row % 4, col % 2
            here = row * COLS + col
            if p != zbits(z)[0]:
                pairs.append((here, (row - z + z + 1 - 2 * (z % 2)) * COLS + col + 1 - 2 * p))
            else:
                pairs.append((here, here))
    return pairs


def body(x_tiles, block_rows, block_cols, pair_left, pair_right, pair_target, branches):
    side_blocks = ROWS * BR
    is_diagonal = (block_rows[0, 0] == block_cols[0, 0]) & (block_rows[0, 0] < side_blocks)
    flags = jnp.pad(is_diagonal.astype(jnp.int32), (0, 2 * DEPTH - SLOTS))
    table = jnp.concatenate([product_table(pair_left[0, 0], pair_right[0, 0], pair_target[0, 0]), flags[None]], axis=0)
    table = lax.ppermute(table, ("row", "col"), partners())
    taken = (branches == 1).astype(jnp.float32)
    coef = jnp.stack([2.0 - 2.0 * taken, 2.0 * taken - 1.0], axis=1)
    purified, terms = run(table, coef, x_tiles[0, 0])
    sums = lax.psum(jnp.sum(terms, axis=(1, 2)), ("row", "col"))
    return (purified[None, None], sums.reshape(STEPS, 2) * (1.0 / (side_blocks * BLK)))


def solution(mesh):
    placed = (
        P("row", "col", None, None, None),
        P("row", "col", None),
        P("row", "col", None),
        P("row", "col", None),
        P("row", "col", None),
        P("row", "col", None),
        P(),
    )
    return jax.shard_map(
        body,
        mesh=mesh,
        in_specs=placed,
        out_specs=(P("row", "col", None, None, None), P()),
        check_vma=False,
    )
```

```python
import jax
import jax.numpy as jnp
from jax import lax
from jax.experimental import pallas as pl
from jax.experimental.pallas import tpu as pltpu
from jax.sharding import PartitionSpec as P

MESH = pl.DeviceIdType.MESH
BR = 3
STEPS = 4
BLK = 128
SLOTS = 12
ROWS = 16
COLS = 8
DEPTH = 32
CHUNKS = 4
CS = SLOTS // CHUNKS
GROUP = 8


def zbits(z):
    low = ((z + 1) // 2) % 2
    high = z // 2
    return low, high


def kernel(
    table, coef, x_hbm, out_hbm, traces, xs, lf, rf, ls, rs, acc, terms, sums, heard,
    r_l, r_r, s_l, s_r, sw_s, sw_r, fin_s, fin_r, t_s, t_r, credit,
):
    row = lax.axis_index("row")
    col = lax.axis_index("col")
    x, z, y, p = row // 4, row % 4, col // 2, col % 2
    low, high = zbits(z)
    moved = p != low

    z_low = z + 1 - 2 * (z % 2)
    z_high = 3 - z
    partner = (x * 4 + z_low, y * 2 + 1 - p)
    sibling = (row, y * 2 + 1 - p)
    l_next = (row, ((y + 1) % 4) * 2 + p)
    l_prev = (row, ((y + 3) % 4) * 2 + p)
    l_pair = (x * 4 + z_low, col)
    r_next = (((x + 1) % 4) * 4 + z, col)
    r_prev = (((x + 3) % 4) * 4 + z, col)
    r_pair = (x * 4 + z_high, col)
    neighbours = (l_next, l_prev, l_pair, r_next, r_prev, r_pair, sibling)

    pairs = (
        (row, (y + 1 - 2 * (y % 2)) * 2 + p),
        (row, (3 - y) * 2 + p),
        l_pair,
        r_pair,
        ((x + 1 - 2 * (x % 2)) * 4 + z, col),
        ((3 - x) * 4 + z, col),
        sibling,
    )

    barrier = pltpu.get_barrier_semaphore()
    for device in neighbours + (partner,):
        pl.semaphore_signal(barrier, inc=1, device_id=device, device_id_type=MESH)
    pl.semaphore_wait(barrier, len(neighbours) + 1)

    def roles(q, h, unit):
        a, b, c = (q + 3) % 4, (q + 1) % 4, (q + 2) % 4
        g = 1 - h
        return [unit(q, h), unit(a, h), unit(b, h), unit(q, g), unit(c, h), unit(a, g), unit(b, g), unit(c, g)]

    units_l = roles(y, low, lambda q, h: q * 2 + h)
    units_r = roles(x, high, lambda q, h: q * 4 + h * 3 + p * (1 - 2 * h))
    units_s = roles(x, high, lambda q, h: q * 4 + h * 3 + (1 - p) * (1 - 2 * h))

    def part(m):
        return pl.ds(m * CS, CS)

    def copy(src, dst, ssem, rsem, device):
        return pltpu.make_async_remote_copy(
            src_ref=src, dst_ref=dst, send_sem=ssem, recv_sem=rsem, device_id=device, device_id_type=MESH
        )

    class Gather:
        def __init__(self, buf, units, rsem, ssem, nxt, prv, pair):
            self.buf, self.units, self.rsem, self.ssem = buf, units, rsem, ssem
            self.nxt, self.prv, self.pair = nxt, prv, pair

        def source(self, role, m):
            return xs.at[part(m)] if role == 0 else self.buf.at[self.units[role], part(m)]

        def plan(self, m):
            nxt, prv, pair = self.nxt, self.prv, self.pair
            first = [(0, nxt, 1), (0, prv, 2), (0, pair, 3)]
            second = [(1, nxt, 4)] if m % 2 == 0 else [(2, prv, 4)]
            if m < CHUNKS // 2:
                second += [(1, pair, 5), (2, pair, 6)]
                third = [(4, pair, 7)]
            else:
                second += [(3, nxt, 5), (3, prv, 6)]
                third = [(5, nxt, 7)] if m % 2 == 0 else [(6, prv, 7)]
            return first, second, third

        def sends(self, m, level):
            plan = self.plan(m)
            at = sum(len(one) for one in plan[:level])
            made = []
            for index, (role, device, there) in enumerate(plan[level]):
                made.append(
                    copy(
                        self.source(role, m),
                        self.buf.at[self.units[role], part(m)],
                        self.ssem.at[m, at + index],
                        self.rsem.at[m, there - 1],
                        device,
                    )
                )
            return made

        def arrived(self, m, role):
            place = self.buf.at[self.units[role], part(m)]
            copy(place, place, self.ssem.at[m, 0], self.rsem.at[m, role - 1], self.nxt).wait_recv()

    left = Gather(lf, units_l, r_l, s_l, l_next, l_prev, l_pair)
    right = Gather(rf, units_r, r_r, s_r, r_next, r_prev, r_pair)

    def share(m, role):
        place = rf.at[units_r[role], part(m)]
        return copy(right.source(role, m), place, s_r.at[m, 7 + role], r_r.at[m, 7 + role], sibling)

    def shared(m, role):
        place = rf.at[units_s[role], part(m)]
        copy(place, place, s_r.at[m, 0], r_r.at[m, 7 + role], sibling).wait_recv()

    def send_own(m):
        for one in left.sends(m, 0) + right.sends(m, 0) + [share(m, 0)]:
            one.start()

    def split(value):
        top = value.astype(jnp.bfloat16)
        return top, (value - top.astype(jnp.float32)).astype(jnp.bfloat16)

    def keep_left(unit, block, value):
        top, low_part = split(value)
        ls[unit * SLOTS + block, 0:BLK] = top
        ls[unit * SLOTS + block, BLK : 2 * BLK] = low_part

    def keep_right(unit, block, value):
        top, low_part = split(value)
        rs[unit * SLOTS + block, :, 0:BLK] = top
        rs[unit * SLOTS + block, :, BLK : 2 * BLK] = low_part

    def prepare_left(m, role):
        unit = units_l[role]

        @pl.loop(m * CS, (m + 1) * CS)
        def _(block):
            keep_left(unit, block, lf[unit, block])

    def prepare_right(m, unit):
        @pl.loop(m * CS, (m + 1) * CS)
        def _(block):
            keep_right(unit, block, rf[unit, block])

    diagonal = lax.broadcasted_iota(jnp.int32, (BLK, BLK), 0) == lax.broadcasted_iota(jnp.int32, (BLK, BLK), 1)

    def folded(value):
        return jnp.sum(value.reshape(BLK // 8, 8, BLK), axis=0)

    def total(step, stage):
        def exchange(index):
            return copy(sums.at[index], heard.at[index], t_s.at[index], t_r.at[index], pairs[index])

        @pl.when(step == STEPS - 1)
        def _():
            if 0 < stage <= len(pairs):
                exchange(stage - 1).wait()
                sums[stage] = sums[stage - 1] + heard[stage - 1]
            if stage < len(pairs):
                exchange(stage).start()
            if stage == len(pairs):
                found = sums[stage]
                for at in range(STEPS):
                    for which in range(2):
                        place = 2 * at + which
                        traces[at, which] = jnp.sum(found[place : place + 1]) * (1.0 / (ROWS * BR * BLK))

    def gather(step):
        def level(m, number, waits):
            for role in waits:
                left.arrived(m, role)
                right.arrived(m, role)
            for one in left.sends(m, number) + right.sends(m, number) + [share(m, role) for role in waits]:
                one.start()

        def prepare(m, waits):
            for role in waits:
                prepare_left(m, role)
                prepare_right(m, units_r[role])

        for m in range(CHUNKS):
            level(m, 1, (1, 2, 3))

        terms[...] = jnp.zeros_like(terms)

        @pl.loop(0, SLOTS)
        def _(block):
            value = xs[block]
            keep_left(units_l[0], block, value)
            keep_right(units_r[0], block, value)
            weight = table[SLOTS, block].astype(jnp.float32)
            terms[0] += folded(jnp.where(diagonal, value, 0.0)) * weight
            terms[1] += folded(value * value)

        for which in range(2):
            sums[0, pl.ds(2 * step + which, 1)] = jnp.sum(terms[which], axis=0, keepdims=True)
        total(step, 0)

        for m in range(CHUNKS):
            prepare(m, (1, 2, 3))
            total(step, 1 + m)
            shared(m, 0)
            prepare_right(m, units_s[0])
        for m in range(CHUNKS):
            level(m, 2, (4, 5, 6))
            total(step, 5 + m)
            for role in (1, 2, 3):
                shared(m, role)
                prepare_right(m, units_s[role])
        for m in range(CHUNKS):
            prepare(m, (4, 5, 6))
            left.arrived(m, 7)
            right.arrived(m, 7)
            share(m, 7).start()
            prepare(m, (7,))
            for role in (4, 5, 6):
                shared(m, role)
                prepare_right(m, units_s[role])
        for m in range(CHUNKS):
            shared(m, 7)
            prepare_right(m, units_s[7])
            for number in range(3):
                for one in left.sends(m, number) + right.sends(m, number):
                    one.wait_send()
            for role in range(8):
                share(m, role).wait_send()

            @pl.when(step < STEPS - 1)
            def _():
                for device in neighbours:
                    pl.semaphore_signal(credit.at[m], inc=1, device_id=device, device_id_type=MESH)

    def multiply(step, m):
        @pl.loop(m * CS, (m + 1) * CS)
        def _(target):
            acc[...] = jnp.zeros_like(acc)

            @pl.loop(0, DEPTH // GROUP)
            def _(turn):
                first = turn * GROUP
                lhs = jnp.concatenate([ls[table[target, first + i]] for i in range(GROUP)], axis=1)
                rhs = jnp.concatenate([rs[table[target, DEPTH + first + i]] for i in range(GROUP)], axis=0)
                acc[...] += jnp.dot(lhs, rhs, preferred_element_type=jnp.float32)

            squared = acc[0:BLK, 0:BLK] + (
                acc[0:BLK, BLK : 2 * BLK] + acc[BLK : 2 * BLK, 0:BLK] + acc[BLK : 2 * BLK, BLK : 2 * BLK]
            )
            stored = xs[target]
            xs[target] = coef[step, 0] * stored + coef[step, 1] * squared

    for m in range(CHUNKS):
        remote = copy(x_hbm.at[part(m)], xs.at[part(m)], sw_s.at[m], sw_r.at[m], partner)
        local = pltpu.make_async_copy(x_hbm.at[part(m)], xs.at[part(m)], sw_r.at[m])
        pl.when(moved)(remote.start)
        pl.when(jnp.logical_not(moved))(local.start)
    sums[...] = jnp.zeros_like(sums)
    ls[COLS * SLOTS] = jnp.zeros((2 * BLK, BLK), jnp.bfloat16)
    for m in range(CHUNKS):
        remote = copy(x_hbm.at[part(m)], xs.at[part(m)], sw_s.at[m], sw_r.at[m], partner)
        local = pltpu.make_async_copy(x_hbm.at[part(m)], xs.at[part(m)], sw_r.at[m])
        pl.when(moved)(remote.wait)
        pl.when(jnp.logical_not(moved))(local.wait)
        send_own(m)

    def finals(m):
        remote = copy(xs.at[part(m)], out_hbm.at[part(m)], fin_s.at[m], fin_r.at[m], partner)
        local = pltpu.make_async_copy(xs.at[part(m)], out_hbm.at[part(m)], fin_r.at[m])
        return remote, local

    @pl.loop(0, STEPS)
    def _(step):
        gather(step)
        for m in range(CHUNKS):
            multiply(step, m)

            @pl.when(step < STEPS - 1)
            def _():
                pl.semaphore_wait(credit.at[m], len(neighbours))
                send_own(m)

            @pl.when(step == STEPS - 1)
            def _():
                remote, local = finals(m)
                pl.when(moved)(remote.start)
                pl.when(jnp.logical_not(moved))(local.start)

    for m in range(CHUNKS):
        remote, local = finals(m)
        pl.when(moved)(remote.wait)
        pl.when(jnp.logical_not(moved))(local.wait)


def run(table, coef, blocks):
    dma = pltpu.SemaphoreType.DMA
    anywhere = pl.BlockSpec(memory_space=pl.ANY)
    scalars = pl.BlockSpec(memory_space=pltpu.SMEM)
    return pl.pallas_call(
        kernel,
        out_shape=(
            jax.ShapeDtypeStruct((SLOTS, BLK, BLK), jnp.float32),
            jax.ShapeDtypeStruct((STEPS, 2), jnp.float32),
        ),
        in_specs=[scalars, scalars, anywhere],
        out_specs=(anywhere, scalars),
        scratch_shapes=[
            pltpu.VMEM((SLOTS, BLK, BLK), jnp.float32),
            pltpu.VMEM((COLS, SLOTS, BLK, BLK), jnp.float32),
            pltpu.VMEM((ROWS, SLOTS, BLK, BLK), jnp.float32),
            pltpu.VMEM((COLS * SLOTS + 1, 2 * BLK, BLK), jnp.bfloat16),
            pltpu.VMEM((ROWS * SLOTS, BLK, 2 * BLK), jnp.bfloat16),
            pltpu.VMEM((2 * BLK, 2 * BLK), jnp.float32),
            pltpu.VMEM((2, 8, BLK), jnp.float32),
            pltpu.VMEM((8, 8, BLK), jnp.float32),
            pltpu.VMEM((7, 8, BLK), jnp.float32),
            dma((CHUNKS, 7)),
            dma((CHUNKS, 15)),
            dma((CHUNKS, 7)),
            dma((CHUNKS, 15)),
            dma((CHUNKS,)),
            dma((CHUNKS,)),
            dma((CHUNKS,)),
            dma((CHUNKS,)),
            dma((7,)),
            dma((7,)),
            pltpu.SemaphoreType.REGULAR((CHUNKS,)),
        ],
        compiler_params=pltpu.CompilerParams(
            collective_id=0, has_side_effects=True, vmem_limit_bytes=52 * 2**20
        ),
        cost_estimate=pl.CostEstimate(
            flops=STEPS * SLOTS * DEPTH * 8 * BLK**3, bytes_accessed=2 * SLOTS * BLK * BLK * 4, transcendentals=0
        ),
    )(table, coef, blocks)


def product_table(left_ids, right_ids, target_ids):
    count = target_ids.shape[0]
    order = jnp.arange(count, dtype=jnp.int32)
    same = (target_ids[:, None] == target_ids[None, :]) & (order[None, :] < order[:, None])
    place = target_ids * DEPTH + jnp.sum(same.astype(jnp.int32), axis=1)
    chosen = place[:, None] == jnp.arange(SLOTS * DEPTH, dtype=jnp.int32)[None, :]
    lefts = jnp.sum(jnp.where(chosen, left_ids[:, None] - COLS * SLOTS, 0), axis=0) + COLS * SLOTS
    rights = jnp.sum(jnp.where(chosen, right_ids[:, None], 0), axis=0)
    return jnp.concatenate([lefts.reshape(SLOTS, DEPTH), rights.reshape(SLOTS, DEPTH)], axis=1)


def partners():
    pairs = []
    for row in range(ROWS):
        for col in range(COLS):
            z, p = row % 4, col % 2
            here = row * COLS + col
            if p != zbits(z)[0]:
                pairs.append((here, (row - z + z + 1 - 2 * (z % 2)) * COLS + col + 1 - 2 * p))
            else:
                pairs.append((here, here))
    return pairs


def body(x_tiles, block_rows, block_cols, pair_left, pair_right, pair_target, branches):
    side_blocks = ROWS * BR
    is_diagonal = (block_rows[0, 0] == block_cols[0, 0]) & (block_rows[0, 0] < side_blocks)
    flags = jnp.pad(is_diagonal.astype(jnp.int32), (0, 2 * DEPTH - SLOTS))
    table = jnp.concatenate([product_table(pair_left[0, 0], pair_right[0, 0], pair_target[0, 0]), flags[None]], axis=0)
    table = lax.ppermute(table, ("row", "col"), partners())
    taken = (branches == 1).astype(jnp.float32)
    coef = jnp.stack([2.0 - 2.0 * taken, 2.0 * taken - 1.0], axis=1)
    purified, traces = run(table, coef, x_tiles[0, 0])
    return (purified[None, None], traces)


def solution(mesh):
    placed = (
        P("row", "col", None, None, None),
        P("row", "col", None),
        P("row", "col", None),
        P("row", "col", None),
        P("row", "col", None),
        P("row", "col", None),
        P(),
    )
    return jax.shard_map(
        body,
        mesh=mesh,
        in_specs=placed,
        out_specs=(P("row", "col", None, None, None), P()),
        check_vma=False,
    )
```

```python
import jax
import jax.numpy as jnp
from jax import lax
from jax.experimental import pallas as pl
from jax.experimental.pallas import tpu as pltpu
from jax.sharding import PartitionSpec as P

MESH = pl.DeviceIdType.MESH
BR = 3
STEPS = 4
BLK = 128
SLOTS = 12
ROWS = 16
COLS = 8
DEPTH = 32
CHUNKS = 6
CS = SLOTS // CHUNKS
RELAYED = 2


def zbits(z):
    low = ((z + 1) // 2) % 2
    high = z // 2
    return low, high


def kernel(
    table, coef, x_hbm, out_hbm, traces, xs, lf, rf, ls, rs, terms, sums, heard,
    r_l, r_r, s_l, s_r, sw_s, sw_r, fin_s, fin_r, t_s, t_r, credit,
):
    row = lax.axis_index("row")
    col = lax.axis_index("col")
    x, z, y, p = row // 4, row % 4, col // 2, col % 2
    low, high = zbits(z)
    moved = p != low

    z_low = z + 1 - 2 * (z % 2)
    z_high = 3 - z
    partner = (x * 4 + z_low, y * 2 + 1 - p)
    sibling = (row, y * 2 + 1 - p)
    l_next = (row, ((y + 1) % 4) * 2 + p)
    l_prev = (row, ((y + 3) % 4) * 2 + p)
    l_pair = (x * 4 + z_low, col)
    r_next = (((x + 1) % 4) * 4 + z, col)
    r_prev = (((x + 3) % 4) * 4 + z, col)
    r_pair = (x * 4 + z_high, col)
    neighbours = (l_next, l_prev, l_pair, r_next, r_prev, r_pair, sibling)

    pairs = (
        (row, (y + 1 - 2 * (y % 2)) * 2 + p),
        (row, (3 - y) * 2 + p),
        l_pair,
        r_pair,
        ((x + 1 - 2 * (x % 2)) * 4 + z, col),
        ((3 - x) * 4 + z, col),
        sibling,
    )

    barrier = pltpu.get_barrier_semaphore()
    for device in neighbours + (partner,):
        pl.semaphore_signal(barrier, inc=1, device_id=device, device_id_type=MESH)
    pl.semaphore_wait(barrier, len(neighbours) + 1)

    def roles(q, h, unit):
        a, b, c = (q + 3) % 4, (q + 1) % 4, (q + 2) % 4
        g = 1 - h
        return [unit(q, h), unit(a, h), unit(b, h), unit(q, g), unit(c, h), unit(a, g), unit(b, g), unit(c, g)]

    units_l = roles(y, low, lambda q, h: q * 2 + h)
    units_r = roles(x, high, lambda q, h: q * 4 + h * 3 + p * (1 - 2 * h))
    units_s = roles(x, high, lambda q, h: q * 4 + h * 3 + (1 - p) * (1 - 2 * h))

    def part(m):
        return pl.ds(m * CS, CS)

    def by_core(zero, one):
        return zero + p * (one - zero)

    def copy(src, dst, ssem, rsem, device):
        return pltpu.make_async_remote_copy(
            src_ref=src, dst_ref=dst, send_sem=ssem, recv_sem=rsem, device_id=device, device_id_type=MESH
        )

    class Gather:
        def __init__(self, buf, units, rsem, ssem, nxt, prv, pair):
            self.buf, self.units, self.rsem, self.ssem = buf, units, rsem, ssem
            self.nxt, self.prv, self.pair = nxt, prv, pair

        def plan(self, m):
            nxt, prv, pair = self.nxt, self.prv, self.pair
            first = [(0, nxt, 1), (0, prv, 2), (0, pair, 3)]
            second = [(1, nxt, 4)] if m % 2 == 0 else [(2, prv, 4)]
            relay = ([(1, pair, 5), (2, pair, 6)], [(4, pair, 7)])
            onward = ([(3, nxt, 5), (3, prv, 6)], [(5, nxt, 7)] if m % 2 == 0 else [(6, prv, 7)])
            unit = lambda sends: [(self.units[role], device, there) for role, device, there in sends]
            if m == RELAYED:
                more = [
                    [(by_core(c, d), (by_core(e[0], f[0]), by_core(e[1], f[1])), there) for (c, e, there), (d, f, _) in both]
                    for both in (zip(unit(onward[0]), unit(relay[0])), zip(unit(onward[1]), unit(relay[1])))
                ]
            else:
                more = [unit(sends) for sends in (relay if m < RELAYED else onward)]
            return unit(first), unit(second) + more[0], more[1]

        def sends(self, m, level):
            plan = self.plan(m)
            at = sum(len(one) for one in plan[:level])
            made = []
            for index, (unit, device, there) in enumerate(plan[level]):
                place = self.buf.at[unit, part(m)]
                source = xs.at[part(m)] if level == 0 else place
                made.append(copy(source, place, self.ssem.at[m, at + index], self.rsem.at[m, there - 1], device))
            return made

        def arrived(self, m, role):
            place = self.buf.at[self.units[role], part(m)]
            copy(place, place, self.ssem.at[m, 0], self.rsem.at[m, role - 1], self.nxt).wait_recv()

    left = Gather(lf, units_l, r_l, s_l, l_next, l_prev, l_pair)
    right = Gather(rf, units_r, r_r, s_r, r_next, r_prev, r_pair)

    def share(m, role):
        place = rf.at[units_r[role], part(m)]
        return copy(xs.at[part(m)] if role == 0 else place, place, s_r.at[m, 7 + role], r_r.at[m, 7 + role], sibling)

    def shared(m, role):
        place = rf.at[units_s[role], part(m)]
        copy(place, place, s_r.at[m, 0], r_r.at[m, 7 + role], sibling).wait_recv()

    def send_own(m):
        for one in left.sends(m, 0) + right.sends(m, 0) + [share(m, 0)]:
            one.start()

    def split(value):
        top = value.astype(jnp.bfloat16)
        return top, (value - top.astype(jnp.float32)).astype(jnp.bfloat16)

    def keep_left(unit, block, value):
        top, low_part = split(value)
        ls[unit * SLOTS + block, 0:BLK] = top
        ls[unit * SLOTS + block, BLK : 2 * BLK] = low_part

    def keep_right(unit, block, value):
        top, low_part = split(value)
        rs[unit * SLOTS + block, :, 0:BLK] = top
        rs[unit * SLOTS + block, :, BLK : 2 * BLK] = low_part

    def prepare_left(m, role):
        unit = units_l[role]

        @pl.loop(m * CS, (m + 1) * CS)
        def _(block):
            keep_left(unit, block, lf[unit, block])

    def prepare_right(m, unit):
        @pl.loop(m * CS, (m + 1) * CS)
        def _(block):
            keep_right(unit, block, rf[unit, block])

    diagonal = lax.broadcasted_iota(jnp.int32, (BLK, BLK), 0) == lax.broadcasted_iota(jnp.int32, (BLK, BLK), 1)

    def folded(value):
        return jnp.sum(value.reshape(BLK // 8, 8, BLK), axis=0)

    def total(step, stage):
        def exchange(index):
            return copy(sums.at[index], heard.at[index], t_s.at[index], t_r.at[index], pairs[index])

        @pl.when(step == STEPS - 1)
        def _():
            if 0 < stage <= len(pairs):
                exchange(stage - 1).wait()
                sums[stage] = sums[stage - 1] + heard[stage - 1]
            if stage < len(pairs):
                exchange(stage).start()
            if stage == len(pairs):
                found = sums[stage]
                for at in range(STEPS):
                    for which in range(2):
                        place = 2 * at + which
                        traces[at, which] = jnp.sum(found[place : place + 1]) * (1.0 / (ROWS * BR * BLK))

    def gather(step):
        def level(m, number, waits):
            for role in waits:
                left.arrived(m, role)
                right.arrived(m, role)
            for one in left.sends(m, number) + right.sends(m, number) + [share(m, role) for role in waits]:
                one.start()

        def prepare(m, waits):
            for role in waits:
                prepare_left(m, role)
                prepare_right(m, units_r[role])

        for m in range(CHUNKS):
            level(m, 1, (1, 2, 3))
            if m == 0:
                prepare_own(step)
            prepare(m, (1, 2, 3))
            shared(m, 0)
            prepare_right(m, units_s[0])
        for m in range(CHUNKS):
            level(m, 2, (4, 5, 6))
            for role in (1, 2, 3):
                shared(m, role)
                prepare_right(m, units_s[role])
            prepare(m, (4, 5, 6))
        for m in range(CHUNKS):
            left.arrived(m, 7)
            right.arrived(m, 7)
            share(m, 7).start()
            prepare(m, (7,))
            for role in (4, 5, 6):
                shared(m, role)
                prepare_right(m, units_s[role])
            if m > 0:
                last_share(m - 1)
                finish(step, m - 1)
        last_share(CHUNKS - 1)

    def last_share(m):
        shared(m, 7)
        prepare_right(m, units_s[7])

    def finish(step, m):
        for number in range(3):
            for one in left.sends(m, number) + right.sends(m, number):
                one.wait_send()
        for role in range(8):
            share(m, role).wait_send()

        @pl.when(step < STEPS - 1)
        def _():
            for device in neighbours:
                pl.semaphore_signal(credit.at[m], inc=1, device_id=device, device_id_type=MESH)

    def prepare_own(step):
        terms[...] = jnp.zeros_like(terms)

        @pl.loop(0, SLOTS)
        def _(block):
            value = xs[block]
            keep_left(units_l[0], block, value)
            keep_right(units_r[0], block, value)
            weight = table[SLOTS, block].astype(jnp.float32)
            terms[0] += folded(jnp.where(diagonal, value, 0.0)) * weight
            terms[1] += folded(value * value)

        for which in range(2):
            sums[0, pl.ds(2 * step + which, 1)] = jnp.sum(terms[which], axis=0, keepdims=True)

    def multiply(step, m):
        @pl.loop(m * CS, (m + 1) * CS)
        def _(target):
            lhs = jnp.concatenate([ls[table[target, i]] for i in range(DEPTH)], axis=1)
            rhs = jnp.concatenate([rs[table[target, DEPTH + i]] for i in range(DEPTH)], axis=0)
            found = jnp.dot(lhs, rhs, preferred_element_type=jnp.float32)
            squared = found[0:BLK, 0:BLK] + (
                found[0:BLK, BLK : 2 * BLK] + found[BLK : 2 * BLK, 0:BLK] + found[BLK : 2 * BLK, BLK : 2 * BLK]
            )
            stored = xs[target]
            xs[target] = coef[step, 0] * stored + coef[step, 1] * squared

    for m in range(CHUNKS):
        remote = copy(x_hbm.at[part(m)], xs.at[part(m)], sw_s.at[m], sw_r.at[m], partner)
        local = pltpu.make_async_copy(x_hbm.at[part(m)], xs.at[part(m)], sw_r.at[m])
        pl.when(moved)(remote.start)
        pl.when(jnp.logical_not(moved))(local.start)
    sums[...] = jnp.zeros_like(sums)
    ls[COLS * SLOTS] = jnp.zeros((2 * BLK, BLK), jnp.bfloat16)
    for m in range(CHUNKS):
        remote = copy(x_hbm.at[part(m)], xs.at[part(m)], sw_s.at[m], sw_r.at[m], partner)
        local = pltpu.make_async_copy(x_hbm.at[part(m)], xs.at[part(m)], sw_r.at[m])
        pl.when(moved)(remote.wait)
        pl.when(jnp.logical_not(moved))(local.wait)
        send_own(m)

    def finals(m):
        remote = copy(xs.at[part(m)], out_hbm.at[part(m)], fin_s.at[m], fin_r.at[m], partner)
        local = pltpu.make_async_copy(xs.at[part(m)], out_hbm.at[part(m)], fin_r.at[m])
        return remote, local

    @pl.loop(0, STEPS)
    def _(step):
        gather(step)
        total(step, 0)
        for m in range(CHUNKS):
            multiply(step, m)
            if m == 0:
                finish(step, CHUNKS - 1)
            total(step, 1 + m)

            @pl.when(step < STEPS - 1)
            def _():
                pl.semaphore_wait(credit.at[m], len(neighbours))
                send_own(m)

            @pl.when(step == STEPS - 1)
            def _():
                remote, local = finals(m)
                pl.when(moved)(remote.start)
                pl.when(jnp.logical_not(moved))(local.start)

    total(STEPS - 1, CHUNKS + 1)
    for m in range(CHUNKS):
        remote, local = finals(m)
        pl.when(moved)(remote.wait)
        pl.when(jnp.logical_not(moved))(local.wait)


def run(table, coef, blocks):
    dma = pltpu.SemaphoreType.DMA
    anywhere = pl.BlockSpec(memory_space=pl.ANY)
    scalars = pl.BlockSpec(memory_space=pltpu.SMEM)
    return pl.pallas_call(
        kernel,
        out_shape=(
            jax.ShapeDtypeStruct((SLOTS, BLK, BLK), jnp.float32),
            jax.ShapeDtypeStruct((STEPS, 2), jnp.float32),
        ),
        in_specs=[scalars, scalars, anywhere],
        out_specs=(anywhere, scalars),
        scratch_shapes=[
            pltpu.VMEM((SLOTS, BLK, BLK), jnp.float32),
            pltpu.VMEM((COLS, SLOTS, BLK, BLK), jnp.float32),
            pltpu.VMEM((ROWS, SLOTS, BLK, BLK), jnp.float32),
            pltpu.VMEM((COLS * SLOTS + 1, 2 * BLK, BLK), jnp.bfloat16),
            pltpu.VMEM((ROWS * SLOTS, BLK, 2 * BLK), jnp.bfloat16),
            pltpu.VMEM((2, 8, BLK), jnp.float32),
            pltpu.VMEM((8, 8, BLK), jnp.float32),
            pltpu.VMEM((7, 8, BLK), jnp.float32),
            dma((CHUNKS, 7)),
            dma((CHUNKS, 15)),
            dma((CHUNKS, 7)),
            dma((CHUNKS, 15)),
            dma((CHUNKS,)),
            dma((CHUNKS,)),
            dma((CHUNKS,)),
            dma((CHUNKS,)),
            dma((7,)),
            dma((7,)),
            pltpu.SemaphoreType.REGULAR((CHUNKS,)),
        ],
        compiler_params=pltpu.CompilerParams(
            collective_id=0, has_side_effects=True, vmem_limit_bytes=52 * 2**20
        ),
        cost_estimate=pl.CostEstimate(
            flops=STEPS * SLOTS * DEPTH * 8 * BLK**3, bytes_accessed=2 * SLOTS * BLK * BLK * 4, transcendentals=0
        ),
    )(table, coef, blocks)


def product_table(left_ids, right_ids, target_ids):
    count = target_ids.shape[0]
    order = jnp.arange(count, dtype=jnp.int32)
    same = (target_ids[:, None] == target_ids[None, :]) & (order[None, :] < order[:, None])
    place = target_ids * DEPTH + jnp.sum(same.astype(jnp.int32), axis=1)
    chosen = place[:, None] == jnp.arange(SLOTS * DEPTH, dtype=jnp.int32)[None, :]
    lefts = jnp.sum(jnp.where(chosen, left_ids[:, None] - COLS * SLOTS, 0), axis=0) + COLS * SLOTS
    rights = jnp.sum(jnp.where(chosen, right_ids[:, None], 0), axis=0)
    return jnp.concatenate([lefts.reshape(SLOTS, DEPTH), rights.reshape(SLOTS, DEPTH)], axis=1)


def partners():
    pairs = []
    for row in range(ROWS):
        for col in range(COLS):
            z, p = row % 4, col % 2
            here = row * COLS + col
            if p != zbits(z)[0]:
                pairs.append((here, (row - z + z + 1 - 2 * (z % 2)) * COLS + col + 1 - 2 * p))
            else:
                pairs.append((here, here))
    return pairs


def body(x_tiles, block_rows, block_cols, pair_left, pair_right, pair_target, branches):
    side_blocks = ROWS * BR
    is_diagonal = (block_rows[0, 0] == block_cols[0, 0]) & (block_rows[0, 0] < side_blocks)
    flags = jnp.pad(is_diagonal.astype(jnp.int32), (0, 2 * DEPTH - SLOTS))
    table = jnp.concatenate([product_table(pair_left[0, 0], pair_right[0, 0], pair_target[0, 0]), flags[None]], axis=0)
    table = lax.ppermute(table, ("row", "col"), partners())
    taken = (branches == 1).astype(jnp.float32)
    coef = jnp.stack([2.0 - 2.0 * taken, 2.0 * taken - 1.0], axis=1)
    purified, traces = run(table, coef, x_tiles[0, 0])
    return (purified[None, None], traces)


def solution(mesh):
    placed = (
        P("row", "col", None, None, None),
        P("row", "col", None),
        P("row", "col", None),
        P("row", "col", None),
        P("row", "col", None),
        P("row", "col", None),
        P(),
    )
    return jax.shard_map(
        body,
        mesh=mesh,
        in_specs=placed,
        out_specs=(P("row", "col", None, None, None), P()),
        check_vma=False,
    )
```

```python
import jax
import jax.numpy as jnp
from jax import lax
from jax.experimental import pallas as pl
from jax.experimental.pallas import tpu as pltpu
from jax.sharding import PartitionSpec as P

MESH = pl.DeviceIdType.MESH
BR = 3
STEPS = 4
BLK = 128
SLOTS = 12
ROWS = 16
COLS = 8
DEPTH = 32
CHUNKS = 6
CS = SLOTS // CHUNKS
VMEM_BYTES = 60 * 2**20
RELAYED = 2


def zbits(z):
    low = ((z + 1) // 2) % 2
    high = z // 2
    return low, high


def kernel(
    branches, rows_hbm, cols_hbm, left_hbm, right_hbm, target_hbm, x_hbm, out_hbm, traces, xs, lf, rf, ls, rs, rows_in, cols_in, left_in, right_in, target_in, lists, built, table, terms, sums, rings,
    r_l, r_r, s_l, s_r, sw_s, sw_r, fin_s, fin_r, t_s, t_r, n_s, n_r, credit,
):
    row = lax.axis_index("row")
    col = lax.axis_index("col")
    x, z, y, p = row // 4, row % 4, col // 2, col % 2
    low, high = zbits(z)
    moved = p != low

    z_low = z + 1 - 2 * (z % 2)
    z_high = 3 - z
    partner = (x * 4 + z_low, y * 2 + 1 - p)
    sibling = (row, y * 2 + 1 - p)
    l_next = (row, ((y + 1) % 4) * 2 + p)
    l_prev = (row, ((y + 3) % 4) * 2 + p)
    l_pair = (x * 4 + z_low, col)
    r_next = (((x + 1) % 4) * 4 + z, col)
    r_prev = (((x + 3) % 4) * 4 + z, col)
    r_pair = (x * 4 + z_high, col)
    neighbours = (l_next, l_prev, l_pair, r_next, r_prev, r_pair, sibling)

    along = (
        (y, [(row, ((y + o) % 4) * 2 + p) for o in (1, 2, 3)]),
        (z, [(x * 4 + (z + o) % 4, col) for o in (1, 2, 3)]),
        (x, [(((x + o) % 4) * 4 + z, col) for o in (1, 2, 3)]),
    )
    greeted = neighbours + (partner,) + tuple(devices[1] for _, devices in along)

    barrier = pltpu.get_barrier_semaphore()
    for device in greeted:
        pl.semaphore_signal(barrier, inc=1, device_id=device, device_id_type=MESH)
    pl.semaphore_wait(barrier, len(greeted))

    def roles(q, h, unit):
        a, b, c = (q + 3) % 4, (q + 1) % 4, (q + 2) % 4
        g = 1 - h
        return [unit(q, h), unit(a, h), unit(b, h), unit(q, g), unit(c, h), unit(a, g), unit(b, g), unit(c, g)]

    units_l = roles(y, low, lambda q, h: q * 2 + h)
    units_r = roles(x, high, lambda q, h: q * 4 + h * 3 + p * (1 - 2 * h))
    units_s = roles(x, high, lambda q, h: q * 4 + h * 3 + (1 - p) * (1 - 2 * h))

    def part(m):
        return pl.ds(m * CS, CS)

    def by_core(zero, one):
        return zero + p * (one - zero)

    def copy(src, dst, ssem, rsem, device):
        return pltpu.make_async_remote_copy(
            src_ref=src, dst_ref=dst, send_sem=ssem, recv_sem=rsem, device_id=device, device_id_type=MESH
        )

    class Gather:
        def __init__(self, buf, units, rsem, ssem, nxt, prv, pair):
            self.buf, self.units, self.rsem, self.ssem = buf, units, rsem, ssem
            self.nxt, self.prv, self.pair = nxt, prv, pair

        def plan(self, m):
            nxt, prv, pair = self.nxt, self.prv, self.pair
            first = [(0, nxt, 1), (0, prv, 2), (0, pair, 3)]
            second = [(1, nxt, 4)] if m % 2 == 0 else [(2, prv, 4)]
            relay = ([(1, pair, 5), (2, pair, 6)], [(4, pair, 7)])
            onward = ([(3, nxt, 5), (3, prv, 6)], [(5, nxt, 7)] if m % 2 == 0 else [(6, prv, 7)])
            unit = lambda sends: [(self.units[role], device, there) for role, device, there in sends]
            ways = [[unit(way[level]) for way in (onward, relay)] for level in range(2)]
            more = []
            for level, (on, back) in enumerate(ways):
                if m == RELAYED or (level == 1 and m == CHUNKS - 1):
                    more.append(
                        [
                            (by_core(c, d), (by_core(e[0], f[0]), by_core(e[1], f[1])), there)
                            for (c, e, there), (d, f, _) in zip(on, back)
                        ]
                    )
                else:
                    more.append(back if m < RELAYED else on)
            return unit(first), unit(second) + more[0], more[1]

        def sends(self, m, level):
            plan = self.plan(m)
            at = sum(len(one) for one in plan[:level])
            made = []
            for index, (unit, device, there) in enumerate(plan[level]):
                place = self.buf.at[unit, part(m)]
                source = xs.at[part(m)] if level == 0 else place
                made.append(copy(source, place, self.ssem.at[m, at + index], self.rsem.at[m, there - 1], device))
            return made

        def arrived(self, m, role):
            place = self.buf.at[self.units[role], part(m)]
            copy(place, place, self.ssem.at[m, 0], self.rsem.at[m, role - 1], self.nxt).wait_recv()

    left = Gather(lf, units_l, r_l, s_l, l_next, l_prev, l_pair)
    right = Gather(rf, units_r, r_r, s_r, r_next, r_prev, r_pair)

    def share(m, role):
        place = rf.at[units_r[role], part(m)]
        return copy(xs.at[part(m)] if role == 0 else place, place, s_r.at[m, 7 + role], r_r.at[m, 7 + role], sibling)

    def shared(m, role):
        place = rf.at[units_s[role], part(m)]
        copy(place, place, s_r.at[m, 0], r_r.at[m, 7 + role], sibling).wait_recv()

    def send_own(m, first=False):
        to_next, to_prev, to_pair = left.sends(m, 0)
        for one in [to_next, to_prev] + right.sends(m, 0) + [share(m, 0)]:
            one.start()
        if first:
            pl.when(jnp.logical_not(moved))(to_pair.start)
        else:
            to_pair.start()

    def split(value):
        top = value.astype(jnp.bfloat16)
        return top, (value - top.astype(jnp.float32)).astype(jnp.bfloat16)

    def keep_left(unit, block, value):
        top, low_part = split(value)
        ls[unit * SLOTS + block, 0:BLK] = top
        ls[unit * SLOTS + block, BLK : 2 * BLK] = low_part

    def keep_right(unit, block, value):
        top, low_part = split(value)
        rs[unit * SLOTS + block, :, 0:BLK] = top
        rs[unit * SLOTS + block, :, BLK : 2 * BLK] = low_part

    def prepare_left(m, role):
        unit = units_l[role]

        @pl.loop(m * CS, (m + 1) * CS)
        def _(block):
            keep_left(unit, block, lf[unit, block])

    def prepare_right(m, unit):
        @pl.loop(m * CS, (m + 1) * CS)
        def _(block):
            keep_right(unit, block, rf[unit, block])

    diagonal = lax.broadcasted_iota(jnp.int32, (BLK, BLK), 0) == lax.broadcasted_iota(jnp.int32, (BLK, BLK), 1)

    def folded(value):
        return jnp.sum(value.reshape(BLK // 8, 8, BLK), axis=0)

    def total(step, stage):
        def core():
            return copy(sums.at[0], sums.at[1], t_s.at[0, 0], t_r.at[0, 0], sibling)

        def ring(index):
            place, devices = along[index]
            mine = rings.at[index, place]
            return [copy(mine, mine, t_s.at[index + 1, o], t_r.at[index + 1, o], devices[o]) for o in range(3)]

        @pl.when(step == STEPS - 1)
        def _():
            if stage == 0:
                core().start()
                return
            if stage == 1:
                core().wait()
                found = sums[0] + sums[1]
            else:
                for one in ring(stage - 2):
                    one.wait()
                found = (rings[stage - 2, 0] + rings[stage - 2, 1]) + (rings[stage - 2, 2] + rings[stage - 2, 3])
            if stage < 4:
                rings[stage - 1, along[stage - 1][0]] = found
                for one in ring(stage - 1):
                    one.start()
                return
            for at in range(STEPS):
                for which in range(2):
                    place = 2 * at + which
                    traces[which, at] = jnp.sum(found[place : place + 1]) * (1.0 / (ROWS * BR * BLK))

    def lists_copies():
        pairs = (
            (rows_hbm, rows_in),
            (cols_hbm, cols_in),
            (left_hbm, left_in),
            (right_hbm, right_in),
            (target_hbm, target_in),
        )
        for at, (src, dst) in enumerate(pairs):
            yield copy(src, dst, n_s.at[at], n_r.at[at], partner), pltpu.make_async_copy(src, dst, n_r.at[at])

    def build_table():
        for remote, local in lists_copies():
            pl.when(moved)(remote.wait)
            pl.when(jnp.logical_not(moved))(local.wait)
        width = SLOTS * DEPTH
        count = target_in.shape[1]
        lists[...] = jnp.full_like(lists, SLOTS)
        lists[0:1, 0:count] = left_in[...]
        lists[1:2, 0:count] = right_in[...]
        lists[2:3, 0:count] = target_in[...]
        same = (rows_in[...] == cols_in[...]) & (rows_in[...] < ROWS * BR)
        built[2:3, 0:SLOTS] = same.astype(jnp.int32)
        given = lists[...]
        lane = lax.broadcasted_iota(jnp.int32, (BLK, width), 1)
        sublane = lax.broadcasted_iota(jnp.int32, (BLK, width), 0)
        starts_at = range(0, width, BLK)

        def column(row, first):
            one = jnp.transpose(jnp.broadcast_to(row[:, first : first + BLK], (BLK, BLK)))
            return jnp.concatenate([one] * (width // BLK), axis=1)

        rank = jnp.zeros((1, width), jnp.int32)
        for first in starts_at:
            earlier = (column(given[2:3], first) == given[2:3]) & (sublane + first < lane)
            rank += jnp.sum(jnp.where(earlier, 1, 0), axis=0, keepdims=True)
        place = given[2:3] * DEPTH + rank
        lefts = jnp.full((1, width), COLS * SLOTS, jnp.int32)
        rights = jnp.zeros((1, width), jnp.int32)
        for first in starts_at:
            chosen = column(place, first) == lane
            lefts += jnp.sum(jnp.where(chosen, column(given[0:1], first) - COLS * SLOTS, 0), axis=0, keepdims=True)
            rights += jnp.sum(jnp.where(chosen, column(given[1:2], first), 0), axis=0, keepdims=True)
        built[0:1] = lefts
        built[1:2] = rights
        done = pltpu.make_async_copy(built, table, n_r.at[5])
        done.start()
        done.wait()

    def gather(step):
        def level(m, number, waits):
            for role in waits:
                left.arrived(m, role)
                right.arrived(m, role)
            for one in left.sends(m, number) + right.sends(m, number) + [share(m, role) for role in waits]:
                one.start()

        def prepare(m, waits):
            for role in waits:
                prepare_left(m, role)
                prepare_right(m, units_r[role])

        for m in range(CHUNKS):
            level(m, 1, (1, 2, 3))
            if m == 0:
                pl.when(step == 0)(build_table)
                prepare_own(step)
                total(step, 0)
            prepare(m, (1, 2, 3))
            shared(m, 0)
            prepare_right(m, units_s[0])
        for m in range(CHUNKS):
            level(m, 2, (4, 5, 6))
            for role in (1, 2, 3):
                shared(m, role)
                prepare_right(m, units_s[role])
            prepare(m, (4, 5, 6))
        for m in range(CHUNKS):
            left.arrived(m, 7)
            right.arrived(m, 7)
            share(m, 7).start()
            prepare(m, (7,))
            for role in (4, 5, 6):
                shared(m, role)
                prepare_right(m, units_s[role])
            if m > 0:
                last_share(m - 1)
                finish(step, m - 1)
        last_share(CHUNKS - 1)

    def last_share(m):
        shared(m, 7)
        prepare_right(m, units_s[7])

    def finish(step, m):
        for number in range(3):
            for one in left.sends(m, number) + right.sends(m, number):
                one.wait_send()
        for role in range(8):
            share(m, role).wait_send()

        @pl.when(step < STEPS - 1)
        def _():
            for device in neighbours:
                pl.semaphore_signal(credit.at[m], inc=1, device_id=device, device_id_type=MESH)

    def prepare_own(step):
        terms[...] = jnp.zeros_like(terms)

        @pl.loop(0, SLOTS)
        def _(block):
            value = xs[block]
            keep_left(units_l[0], block, value)
            keep_right(units_r[0], block, value)
            weight = table[2, block].astype(jnp.float32)
            terms[0] += folded(jnp.where(diagonal, value, 0.0)) * weight
            terms[1] += folded(value * value)

        for which in range(2):
            sums[0, pl.ds(2 * step + which, 1)] = jnp.sum(terms[which], axis=0, keepdims=True)

    def multiply(step, m):
        @pl.loop(m * CS, (m + 1) * CS)
        def _(target):
            lhs = jnp.concatenate([ls[table[0, target * DEPTH + i]] for i in range(DEPTH)], axis=1)
            rhs = jnp.concatenate([rs[table[1, target * DEPTH + i]] for i in range(DEPTH)], axis=0)
            found = jnp.dot(lhs, rhs, preferred_element_type=jnp.float32)
            squared = found[0:BLK, 0:BLK] + (
                found[0:BLK, BLK : 2 * BLK] + found[BLK : 2 * BLK, 0:BLK] + found[BLK : 2 * BLK, BLK : 2 * BLK]
            )
            stored = xs[target]
            taken = (branches[step] == 1).astype(jnp.float32)
            xs[target] = (2.0 - 2.0 * taken) * stored + (2.0 * taken - 1.0) * squared

    def starts(m):
        remote = copy(x_hbm.at[part(m)], xs.at[part(m)], sw_s.at[m], sw_r.at[m], partner)
        local = pltpu.make_async_copy(x_hbm.at[part(m)], xs.at[part(m)], sw_r.at[m])
        return remote, local

    def beside(m):
        return copy(x_hbm.at[part(m)], lf.at[units_l[3], part(m)], s_l.at[m, 2], r_l.at[m, 2], sibling)

    for m in range(CHUNKS):
        remote, local = starts(m)
        pl.when(moved)(remote.start)
        pl.when(moved)(beside(m).start)
        pl.when(jnp.logical_not(moved))(local.start)
    for remote, local in lists_copies():
        pl.when(moved)(remote.start)
        pl.when(jnp.logical_not(moved))(local.start)
    sums[...] = jnp.zeros_like(sums)
    built[...] = jnp.zeros_like(built)
    ls[COLS * SLOTS] = jnp.zeros((2 * BLK, BLK), jnp.bfloat16)
    for m in range(CHUNKS):
        remote, local = starts(m)
        pl.when(moved)(remote.wait)
        pl.when(jnp.logical_not(moved))(local.wait)
        send_own(m, first=True)

    def finals(m):
        remote = copy(xs.at[part(m)], out_hbm.at[part(m)], fin_s.at[m], fin_r.at[m], partner)
        local = pltpu.make_async_copy(xs.at[part(m)], out_hbm.at[part(m)], fin_r.at[m])
        return remote, local

    @pl.loop(0, STEPS)
    def _(step):
        gather(step)
        total(step, 1)
        for m in range(CHUNKS):
            multiply(step, m)
            if m == 0:
                finish(step, CHUNKS - 1)
            if m % 2 == 1:
                total(step, 2 + m // 2)

            @pl.when(step < STEPS - 1)
            def _():
                pl.semaphore_wait(credit.at[m], len(neighbours))
                send_own(m)

            @pl.when(step == STEPS - 1)
            def _():
                remote, local = finals(m)
                pl.when(moved)(remote.start)
                pl.when(jnp.logical_not(moved))(local.start)

    for m in range(CHUNKS):
        remote, local = finals(m)
        pl.when(moved)(remote.wait)
        pl.when(jnp.logical_not(moved))(local.wait)


def run(branches, rows, cols, lefts, rights, targets, blocks):
    dma = pltpu.SemaphoreType.DMA
    anywhere = pl.BlockSpec(memory_space=pl.ANY)
    scalars = pl.BlockSpec(memory_space=pltpu.SMEM)
    width = SLOTS * DEPTH
    count = targets.shape[1]
    return pl.pallas_call(
        kernel,
        out_shape=(
            jax.ShapeDtypeStruct((SLOTS, BLK, BLK), jnp.float32),
            jax.ShapeDtypeStruct((2, STEPS), jnp.float32),
        ),
        in_specs=[scalars] + [anywhere] * 6,
        out_specs=(anywhere, scalars),
        scratch_shapes=[
            pltpu.VMEM((SLOTS, BLK, BLK), jnp.float32),
            pltpu.VMEM((COLS, SLOTS, BLK, BLK), jnp.float32),
            pltpu.VMEM((ROWS, SLOTS, BLK, BLK), jnp.float32),
            pltpu.VMEM((COLS * SLOTS + 1, 2 * BLK, BLK), jnp.bfloat16),
            pltpu.VMEM((ROWS * SLOTS, BLK, 2 * BLK), jnp.bfloat16),
            pltpu.VMEM((1, SLOTS), jnp.int32),
            pltpu.VMEM((1, SLOTS), jnp.int32),
            pltpu.VMEM((1, count), jnp.int32),
            pltpu.VMEM((1, count), jnp.int32),
            pltpu.VMEM((1, count), jnp.int32),
            pltpu.VMEM((8, width), jnp.int32),
            pltpu.VMEM((8, width), jnp.int32),
            pltpu.SMEM((8, width), jnp.int32),
            pltpu.VMEM((2, 8, BLK), jnp.float32),
            pltpu.VMEM((2, 8, BLK), jnp.float32),
            pltpu.VMEM((3, 4, 8, BLK), jnp.float32),
            dma((CHUNKS, 7)),
            dma((CHUNKS, 15)),
            dma((CHUNKS, 7)),
            dma((CHUNKS, 15)),
            dma((CHUNKS,)),
            dma((CHUNKS,)),
            dma((CHUNKS,)),
            dma((CHUNKS,)),
            dma((4, 3)),
            dma((4, 3)),
            dma((5,)),
            dma((6,)),
            pltpu.SemaphoreType.REGULAR((CHUNKS,)),
        ],
        compiler_params=pltpu.CompilerParams(
            collective_id=0, has_side_effects=True, vmem_limit_bytes=VMEM_BYTES
        ),
        cost_estimate=pl.CostEstimate(
            flops=STEPS * SLOTS * DEPTH * 8 * BLK**3, bytes_accessed=2 * SLOTS * BLK * BLK * 4, transcendentals=0
        ),
    )(branches, rows, cols, lefts, rights, targets, blocks)


def body(x_tiles, block_rows, block_cols, pair_left, pair_right, pair_target, branches):
    purified, traces = run(
        branches, block_rows[0], block_cols[0], pair_left[0], pair_right[0], pair_target[0], x_tiles[0, 0]
    )
    return (purified[None, None], traces.T)


def solution(mesh):
    placed = (
        P("row", "col", None, None, None),
        P("row", "col", None),
        P("row", "col", None),
        P("row", "col", None),
        P("row", "col", None),
        P("row", "col", None),
        P(),
    )
    return jax.shard_map(
        body,
        mesh=mesh,
        in_specs=placed,
        out_specs=(P("row", "col", None, None, None), P()),
        check_vma=False,
    )
```

```python
import jax
import jax.numpy as jnp
from jax import lax
from jax.experimental import pallas as pl
from jax.experimental.pallas import tpu as pltpu
from jax.sharding import PartitionSpec as P

MESH = pl.DeviceIdType.MESH
BR = 3
STEPS = 4
BLK = 128
SLOTS = 12
ROWS = 16
COLS = 8
DEPTH = 32
SIZES = (1, 2, 3, 3, 2, 1)
CHUNKS = len(SIZES)
STARTS = tuple(sum(SIZES[:m]) for m in range(CHUNKS))
VMEM_BYTES = 60 * 2**20
FORWARD = (2, 3)
RELAYED = (1, 2)
RELAYED_LAST = 5


def zbits(z):
    low = ((z + 1) // 2) % 2
    high = z // 2
    return low, high


def kernel(
    branches, rows_hbm, cols_hbm, left_hbm, right_hbm, target_hbm, x_hbm, out_hbm, traces, xs, lf, rf, ls, rs, rows_in, cols_in, left_in, right_in, target_in, lists, built, table, terms, sums, rings,
    r_l, r_r, s_l, s_r, sw_s, sw_r, fin_s, fin_r, t_s, t_r, n_s, n_r, credit,
):
    row = lax.axis_index("row")
    col = lax.axis_index("col")
    x, z, y, p = row // 4, row % 4, col // 2, col % 2
    low, high = zbits(z)
    moved = p != low

    z_low = z + 1 - 2 * (z % 2)
    z_high = 3 - z
    partner = (x * 4 + z_low, y * 2 + 1 - p)
    sibling = (row, y * 2 + 1 - p)
    l_next = (row, ((y + 1) % 4) * 2 + p)
    l_prev = (row, ((y + 3) % 4) * 2 + p)
    l_pair = (x * 4 + z_low, col)
    r_next = (((x + 1) % 4) * 4 + z, col)
    r_prev = (((x + 3) % 4) * 4 + z, col)
    r_pair = (x * 4 + z_high, col)
    neighbours = (l_next, l_prev, l_pair, r_next, r_prev, r_pair, sibling)

    along = (
        (y, [(row, ((y + o) % 4) * 2 + p) for o in (1, 2, 3)]),
        (z, [(x * 4 + (z + o) % 4, col) for o in (1, 2, 3)]),
        (x, [(((x + o) % 4) * 4 + z, col) for o in (1, 2, 3)]),
    )
    greeted = neighbours + (partner,) + tuple(devices[1] for _, devices in along)

    def part(m):
        return pl.ds(STARTS[m], SIZES[m])

    def slots(m):
        return pl.loop(STARTS[m], STARTS[m] + SIZES[m])

    def copy(src, dst, ssem, rsem, device):
        return pltpu.make_async_remote_copy(
            src_ref=src, dst_ref=dst, send_sem=ssem, recv_sem=rsem, device_id=device, device_id_type=MESH
        )

    def starts(m):
        return copy(x_hbm.at[part(m)], xs.at[part(m)], sw_s.at[m], sw_r.at[m], partner)

    def starts_here(m):
        return pltpu.make_async_copy(x_hbm.at[part(m)], xs.at[part(m)], sw_r.at[m])

    for m in range(CHUNKS):
        pl.when(jnp.logical_not(moved))(starts_here(m).start)
    ls[COLS * SLOTS] = jnp.zeros((2 * BLK, BLK), jnp.bfloat16)
    sums[...] = jnp.zeros_like(sums)
    built[...] = jnp.zeros_like(built)

    barrier = pltpu.get_barrier_semaphore()
    for device in greeted:
        pl.semaphore_signal(barrier, inc=1, device_id=device, device_id_type=MESH)
    pl.semaphore_wait(barrier, len(greeted))

    def roles(q, h, unit):
        a, b, c = (q + 3) % 4, (q + 1) % 4, (q + 2) % 4
        g = 1 - h
        return [unit(q, h), unit(a, h), unit(b, h), unit(q, g), unit(c, h), unit(a, g), unit(b, g), unit(c, g)]

    units_l = roles(y, low, lambda q, h: q * 2 + h)
    units_r = roles(x, high, lambda q, h: q * 4 + h * 3 + p * (1 - 2 * h))
    units_s = roles(x, high, lambda q, h: q * 4 + h * 3 + (1 - p) * (1 - 2 * h))

    def by_core(zero, one):
        return zero + p * (one - zero)

    class Gather:
        def __init__(self, buf, units, rsem, ssem, nxt, prv, pair):
            self.buf, self.units, self.rsem, self.ssem = buf, units, rsem, ssem
            self.nxt, self.prv, self.pair = nxt, prv, pair

        def plan(self, m):
            nxt, prv, pair = self.nxt, self.prv, self.pair
            ahead = m in FORWARD
            first = [(0, nxt, 1), (0, prv, 2), (0, pair, 3)]
            opposite = (1, nxt, 4) if ahead else (2, prv, 4)
            unit = lambda sends: [(self.units[role], device, there) for role, device, there in sends]
            if m in RELAYED:
                return [unit(sends) for sends in (first, [opposite, (1, pair, 5), (2, pair, 6)], [], [(4, pair, 7)])]
            to_next, to_prev = (3, nxt, 5), (3, prv, 6)
            on, end = (to_next, to_prev) if ahead else (to_prev, to_next)
            last = (5, nxt, 7) if ahead else (6, prv, 7)
            if m != RELAYED_LAST:
                return [unit(sends) for sends in (first, [on], [opposite, end], [last])]
            return [unit(sends) for sends in (first, [on, opposite], [end], [(4, pair, 7)])]

        def sent_on(self, m):
            if m in RELAYED:
                return (4,)
            return (4,) if m == RELAYED_LAST else ((5,) if m in FORWARD else (6,))

        def sends(self, m, level):
            plan = self.plan(m)
            at = sum(len(one) for one in plan[:level])
            made = []
            for index, (unit, device, there) in enumerate(plan[level]):
                place = self.buf.at[unit, part(m)]
                source = xs.at[part(m)] if level == 0 else place
                made.append(copy(source, place, self.ssem.at[m, at + index], self.rsem.at[m, there - 1], device))
            return made

        def arrived(self, m, role):
            place = self.buf.at[self.units[role], part(m)]
            copy(place, place, self.ssem.at[m, 0], self.rsem.at[m, role - 1], self.nxt).wait_recv()

    left = Gather(lf, units_l, r_l, s_l, l_next, l_prev, l_pair)
    right = Gather(rf, units_r, r_r, s_r, r_next, r_prev, r_pair)

    def share(m, role):
        place = rf.at[units_r[role], part(m)]
        return copy(xs.at[part(m)] if role == 0 else place, place, s_r.at[m, 7 + role], r_r.at[m, 7 + role], sibling)

    def shared(m, role):
        place = rf.at[units_s[role], part(m)]
        copy(place, place, s_r.at[m, 0], r_r.at[m, 7 + role], sibling).wait_recv()

    def send_own(m, first=False):
        to_next, to_prev, to_pair = left.sends(m, 0)
        for one in [to_next, to_prev] + right.sends(m, 0) + [share(m, 0)]:
            one.start()
        if first:
            pl.when(jnp.logical_not(moved))(to_pair.start)
        else:
            to_pair.start()

    def split(value):
        top = value.astype(jnp.bfloat16)
        return top, (value - top.astype(jnp.float32)).astype(jnp.bfloat16)

    def keep_left(unit, block, value):
        top, low_part = split(value)
        ls[unit * SLOTS + block, 0:BLK] = top
        ls[unit * SLOTS + block, BLK : 2 * BLK] = low_part

    def keep_right(unit, block, value):
        top, low_part = split(value)
        rs[unit * SLOTS + block, :, 0:BLK] = top
        rs[unit * SLOTS + block, :, BLK : 2 * BLK] = low_part

    def prepare_left(m, role):
        unit = units_l[role]

        @slots(m)
        def _(block):
            keep_left(unit, block, lf[unit, block])

    def prepare_right(m, unit):
        @slots(m)
        def _(block):
            keep_right(unit, block, rf[unit, block])

    diagonal = lax.broadcasted_iota(jnp.int32, (BLK, BLK), 0) == lax.broadcasted_iota(jnp.int32, (BLK, BLK), 1)

    def folded(value):
        return jnp.sum(value.reshape(BLK // 8, 8, BLK), axis=0)

    def total(step, stage):
        def core():
            return copy(sums.at[0], sums.at[1], t_s.at[0, 0], t_r.at[0, 0], sibling)

        def ring(index):
            place, devices = along[index]
            mine = rings.at[index, place]
            return [copy(mine, mine, t_s.at[index + 1, o], t_r.at[index + 1, o], devices[o]) for o in range(3)]

        @pl.when(step == STEPS - 1)
        def _():
            if stage == 0:
                core().start()
                return
            if stage == 1:
                core().wait()
                found = sums[0] + sums[1]
            else:
                for one in ring(stage - 2):
                    one.wait()
                found = (rings[stage - 2, 0] + rings[stage - 2, 1]) + (rings[stage - 2, 2] + rings[stage - 2, 3])
            if stage < 4:
                rings[stage - 1, along[stage - 1][0]] = found
                for one in ring(stage - 1):
                    one.start()
                return
            for at in range(STEPS):
                for which in range(2):
                    place = 2 * at + which
                    traces[which, at] = jnp.sum(found[place : place + 1]) * (1.0 / (ROWS * BR * BLK))

    def lists_copies():
        pairs = (
            (rows_hbm, rows_in),
            (cols_hbm, cols_in),
            (left_hbm, left_in),
            (right_hbm, right_in),
            (target_hbm, target_in),
        )
        for at, (src, dst) in enumerate(pairs):
            yield copy(src, dst, n_s.at[at], n_r.at[at], partner), pltpu.make_async_copy(src, dst, n_r.at[at])

    def build_table():
        for remote, local in lists_copies():
            pl.when(moved)(remote.wait)
            pl.when(jnp.logical_not(moved))(local.wait)
        width = SLOTS * DEPTH
        count = target_in.shape[1]
        lists[...] = jnp.full_like(lists, SLOTS)
        lists[0:1, 0:count] = left_in[...]
        lists[1:2, 0:count] = right_in[...]
        lists[2:3, 0:count] = target_in[...]
        same = (rows_in[...] == cols_in[...]) & (rows_in[...] < ROWS * BR)
        built[2:3, 0:SLOTS] = same.astype(jnp.int32)
        given = lists[...]
        lane = lax.broadcasted_iota(jnp.int32, (BLK, width), 1)
        sublane = lax.broadcasted_iota(jnp.int32, (BLK, width), 0)
        starts_at = range(0, width, BLK)

        def column(row, first):
            one = jnp.transpose(jnp.broadcast_to(row[:, first : first + BLK], (BLK, BLK)))
            return jnp.concatenate([one] * (width // BLK), axis=1)

        rank = jnp.zeros((1, width), jnp.int32)
        for first in starts_at:
            earlier = (column(given[2:3], first) == given[2:3]) & (sublane + first < lane)
            rank += jnp.sum(jnp.where(earlier, 1, 0), axis=0, keepdims=True)
        place = given[2:3] * DEPTH + rank
        lefts = jnp.full((1, width), COLS * SLOTS, jnp.int32)
        rights = jnp.zeros((1, width), jnp.int32)
        for first in starts_at:
            chosen = column(place, first) == lane
            lefts += jnp.sum(jnp.where(chosen, column(given[0:1], first) - COLS * SLOTS, 0), axis=0, keepdims=True)
            rights += jnp.sum(jnp.where(chosen, column(given[1:2], first), 0), axis=0, keepdims=True)
        built[0:1] = lefts
        built[1:2] = rights
        done = pltpu.make_async_copy(built, table, n_r.at[5])
        done.start()
        done.wait()

    def gather(step):
        def arrive(m, waits):
            for role in waits:
                left.arrived(m, role)
                right.arrived(m, role)

        def send(m, number):
            for one in left.sends(m, number) + right.sends(m, number):
                one.start()

        def share_all(m, waits):
            for role in waits:
                share(m, role).start()

        def prepare(m, waits):
            for role in waits:
                prepare_left(m, role)
                prepare_right(m, units_r[role])

        def prepare_shared(m, waits):
            for role in waits:
                shared(m, role)
                prepare_right(m, units_s[role])

        for m in range(CHUNKS):
            arrive(m, (1, 2, 3))
            send(m, 1)
            if m == CHUNKS - 1:
                for after in range(CHUNKS):
                    send(after, 2)
            share_all(m, (1, 2, 3))
            if m == 0:
                pl.when(step == 0)(build_table)
                prepare_own(step)
                total(step, 0)
            prepare(m, (1, 2, 3))
            prepare_shared(m, (0,))
        for m in range(CHUNKS):
            roles_now = left.sent_on(m)
            arrive(m, roles_now)
            send(m, 3)
            share_all(m, roles_now)
            prepare(m, roles_now)
            prepare_shared(m, (1, 2, 3))
        def take(m, waits):
            for role in waits:
                right.arrived(m, role)
                share(m, role).start()
            for role in waits:
                left.arrived(m, role)
            prepare(m, waits)

        for m in range(CHUNKS):
            take(m, [role for role in (4, 5, 6) if role not in left.sent_on(m)])
        for m in range(CHUNKS):
            right.arrived(m, 7)
            share(m, 7).start()
            prepare_right(m, units_r[7])
            prepare_shared(m, (4, 5, 6))
            if m > 0:
                last_share(m - 1)
            if m == CHUNKS - 2:
                pl.when(step < STEPS - 1)(lambda: finish(0))
        for m in range(CHUNKS):
            left.arrived(m, 7)
            prepare_left(m, 7)
        last_share(CHUNKS - 1)

    def last_share(m):
        shared(m, 7)
        prepare_right(m, units_s[7])

    def sent_own(m):
        for one in left.sends(m, 0) + right.sends(m, 0) + [share(m, 0)]:
            one.wait_send()

    def sent_rest(m):
        for number in range(1, 4):
            for one in left.sends(m, number) + right.sends(m, number):
                one.wait_send()
        for role in range(1, 8):
            share(m, role).wait_send()

    def finish(m):
        sent_own(m)
        sent_rest(m)
        for device in neighbours:
            pl.semaphore_signal(credit.at[m], inc=1, device_id=device, device_id_type=MESH)

    def prepare_own(step):
        terms[...] = jnp.zeros_like(terms)

        @pl.loop(0, SLOTS)
        def _(block):
            value = xs[block]
            keep_left(units_l[0], block, value)
            keep_right(units_r[0], block, value)
            weight = table[2, block].astype(jnp.float32)
            terms[0] += folded(jnp.where(diagonal, value, 0.0)) * weight
            terms[1] += folded(value * value)

        for which in range(2):
            sums[0, pl.ds(2 * step + which, 1)] = jnp.sum(terms[which], axis=0, keepdims=True)

    def multiply(step, m):
        @slots(m)
        def _(target):
            lhs = jnp.concatenate([ls[table[0, target * DEPTH + i]] for i in range(DEPTH)], axis=1)
            rhs = jnp.concatenate([rs[table[1, target * DEPTH + i]] for i in range(DEPTH)], axis=0)
            found = jnp.dot(lhs, rhs, preferred_element_type=jnp.float32)
            squared = found[0:BLK, 0:BLK] + (
                found[0:BLK, BLK : 2 * BLK] + found[BLK : 2 * BLK, 0:BLK] + found[BLK : 2 * BLK, BLK : 2 * BLK]
            )
            stored = xs[target]
            taken = (branches[step] == 1).astype(jnp.float32)
            xs[target] = (2.0 - 2.0 * taken) * stored + (2.0 * taken - 1.0) * squared

    def beside(m):
        return copy(x_hbm.at[part(m)], lf.at[units_l[3], part(m)], s_l.at[m, 2], r_l.at[m, 2], sibling)

    for m in range(CHUNKS):
        pl.when(moved)(starts(m).start)
        pl.when(moved)(beside(m).start)
    for remote, local in lists_copies():
        pl.when(moved)(remote.start)
        pl.when(jnp.logical_not(moved))(local.start)
    for m in range(CHUNKS):
        pl.when(moved)(starts(m).wait)
        pl.when(jnp.logical_not(moved))(starts_here(m).wait)
        send_own(m, first=True)

    def finals(m):
        remote = copy(xs.at[part(m)], out_hbm.at[part(m)], fin_s.at[m], fin_r.at[m], partner)
        local = pltpu.make_async_copy(xs.at[part(m)], out_hbm.at[part(m)], fin_r.at[m])
        return remote, local

    @pl.loop(0, STEPS)
    def _(step):
        gather(step)
        total(step, 1)
        for m in range(CHUNKS):
            pl.when(step == STEPS - 1)(lambda m=m: sent_own(m))
            multiply(step, m)

            @pl.when(step < STEPS - 1)
            def _():
                pl.semaphore_wait(credit.at[m], len(neighbours))
                send_own(m)
                if m + 1 < CHUNKS:
                    finish(m + 1)

            @pl.when(step == STEPS - 1)
            def _():
                remote, local = finals(m)
                pl.when(moved)(remote.start)
                pl.when(jnp.logical_not(moved))(local.start)

            if m % 2 == 1:
                total(step, 2 + m // 2)

    for m in range(CHUNKS):
        sent_rest(m)
        remote, local = finals(m)
        pl.when(moved)(remote.wait)
        pl.when(jnp.logical_not(moved))(local.wait)


def run(branches, rows, cols, lefts, rights, targets, blocks):
    dma = pltpu.SemaphoreType.DMA
    main = pl.BlockSpec(memory_space=pltpu.HBM)
    scalars = pl.BlockSpec(memory_space=pltpu.SMEM)
    width = SLOTS * DEPTH
    count = targets.shape[1]
    return pl.pallas_call(
        kernel,
        out_shape=(
            jax.ShapeDtypeStruct((SLOTS, BLK, BLK), jnp.float32),
            jax.ShapeDtypeStruct((2, STEPS), jnp.float32),
        ),
        in_specs=[scalars] + [main] * 6,
        out_specs=(main, scalars),
        scratch_shapes=[
            pltpu.VMEM((SLOTS, BLK, BLK), jnp.float32),
            pltpu.VMEM((COLS, SLOTS, BLK, BLK), jnp.float32),
            pltpu.VMEM((ROWS, SLOTS, BLK, BLK), jnp.float32),
            pltpu.VMEM((COLS * SLOTS + 1, 2 * BLK, BLK), jnp.bfloat16),
            pltpu.VMEM((ROWS * SLOTS, BLK, 2 * BLK), jnp.bfloat16),
            pltpu.VMEM((1, SLOTS), jnp.int32),
            pltpu.VMEM((1, SLOTS), jnp.int32),
            pltpu.VMEM((1, count), jnp.int32),
            pltpu.VMEM((1, count), jnp.int32),
            pltpu.VMEM((1, count), jnp.int32),
            pltpu.VMEM((8, width), jnp.int32),
            pltpu.VMEM((8, width), jnp.int32),
            pltpu.SMEM((8, width), jnp.int32),
            pltpu.VMEM((2, 8, BLK), jnp.float32),
            pltpu.VMEM((2, 8, BLK), jnp.float32),
            pltpu.VMEM((3, 4, 8, BLK), jnp.float32),
            dma((CHUNKS, 7)),
            dma((CHUNKS, 15)),
            dma((CHUNKS, 7)),
            dma((CHUNKS, 15)),
            dma((CHUNKS,)),
            dma((CHUNKS,)),
            dma((CHUNKS,)),
            dma((CHUNKS,)),
            dma((4, 3)),
            dma((4, 3)),
            dma((5,)),
            dma((6,)),
            pltpu.SemaphoreType.REGULAR((CHUNKS,)),
        ],
        compiler_params=pltpu.CompilerParams(
            collective_id=0, has_side_effects=True, vmem_limit_bytes=VMEM_BYTES
        ),
        cost_estimate=pl.CostEstimate(
            flops=STEPS * SLOTS * DEPTH * 8 * BLK**3, bytes_accessed=2 * SLOTS * BLK * BLK * 4, transcendentals=0
        ),
    )(branches, rows, cols, lefts, rights, targets, blocks)


def body(x_tiles, block_rows, block_cols, pair_left, pair_right, pair_target, branches):
    purified, traces = run(
        branches, block_rows[0], block_cols[0], pair_left[0], pair_right[0], pair_target[0], x_tiles[0, 0]
    )
    return (purified[None, None], traces.T)


def solution(mesh):
    placed = (
        P("row", "col", None, None, None),
        P("row", "col", None),
        P("row", "col", None),
        P("row", "col", None),
        P("row", "col", None),
        P("row", "col", None),
        P(),
    )
    return jax.shard_map(
        body,
        mesh=mesh,
        in_specs=placed,
        out_specs=(P("row", "col", None, None, None), P()),
        check_vma=False,
    )
```

```python
import jax
import jax.numpy as jnp
from jax import lax
from jax.experimental import pallas as pl
from jax.experimental.pallas import tpu as pltpu
from jax.sharding import PartitionSpec as P

MESH = pl.DeviceIdType.MESH
BR = 3
STEPS = 4
BLK = 128
SLOTS = 12
ROWS = 16
COLS = 8
DEPTH = 32
SIZES = (1, 2, 3, 3, 2, 1)
CHUNKS = len(SIZES)
STARTS = tuple(sum(SIZES[:m]) for m in range(CHUNKS))
VMEM_BYTES = 60 * 2**20
FORWARD = (2, 3)
RELAYED = (1, 2)
RELAYED_LAST = 5


def zbits(z):
    low = ((z + 1) // 2) % 2
    high = z // 2
    return low, high


def kernel(
    branches, rows_hbm, cols_hbm, left_hbm, right_hbm, target_hbm, x_hbm, out_hbm, traces, xs, lf, rf, ls, rs, rows_in, cols_in, left_in, right_in, target_in, lists, built, table, terms, sums, rings,
    r_l, r_r, s_l, s_r, sw_s, sw_r, fin_s, fin_r, t_s, t_r, n_s, n_r, credit,
):
    row = lax.axis_index("row")
    col = lax.axis_index("col")
    x, z, y, p = row // 4, row % 4, col // 2, col % 2
    low, high = zbits(z)
    moved = p != low

    z_low = z + 1 - 2 * (z % 2)
    z_high = 3 - z
    partner = (x * 4 + z_low, y * 2 + 1 - p)
    sibling = (row, y * 2 + 1 - p)
    l_next = (row, ((y + 1) % 4) * 2 + p)
    l_prev = (row, ((y + 3) % 4) * 2 + p)
    l_pair = (x * 4 + z_low, col)
    r_next = (((x + 1) % 4) * 4 + z, col)
    r_prev = (((x + 3) % 4) * 4 + z, col)
    r_pair = (x * 4 + z_high, col)
    neighbours = (l_next, l_prev, l_pair, r_next, r_prev, r_pair, sibling)

    along = (
        (y, [(row, ((y + o) % 4) * 2 + p) for o in (1, 2, 3)]),
        (z, [(x * 4 + (z + o) % 4, col) for o in (1, 2, 3)]),
        (x, [(((x + o) % 4) * 4 + z, col) for o in (1, 2, 3)]),
    )
    greeted = neighbours + (partner,) + tuple(devices[1] for _, devices in along)

    def part(m):
        return pl.ds(STARTS[m], SIZES[m])

    def slots(m):
        return pl.loop(STARTS[m], STARTS[m] + SIZES[m])

    def copy(src, dst, ssem, rsem, device):
        return pltpu.make_async_remote_copy(
            src_ref=src, dst_ref=dst, send_sem=ssem, recv_sem=rsem, device_id=device, device_id_type=MESH
        )

    def starts(m):
        return copy(x_hbm.at[part(m)], xs.at[part(m)], sw_s.at[m], sw_r.at[m], partner)

    def starts_here(m):
        return pltpu.make_async_copy(x_hbm.at[part(m)], xs.at[part(m)], sw_r.at[m])

    for m in range(CHUNKS):
        pl.when(jnp.logical_not(moved))(starts_here(m).start)
    ls[COLS * SLOTS] = jnp.zeros((2 * BLK, BLK), jnp.bfloat16)
    sums[...] = jnp.zeros_like(sums)
    built[...] = jnp.zeros_like(built)

    barrier = pltpu.get_barrier_semaphore()
    for device in greeted:
        pl.semaphore_signal(barrier, inc=1, device_id=device, device_id_type=MESH)
    pl.semaphore_wait(barrier, len(greeted))

    def roles(q, h, unit):
        a, b, c = (q + 3) % 4, (q + 1) % 4, (q + 2) % 4
        g = 1 - h
        return [unit(q, h), unit(a, h), unit(b, h), unit(q, g), unit(c, h), unit(a, g), unit(b, g), unit(c, g)]

    units_l = roles(y, low, lambda q, h: q * 2 + h)
    units_r = roles(x, high, lambda q, h: q * 4 + h * 3 + p * (1 - 2 * h))
    units_s = roles(x, high, lambda q, h: q * 4 + h * 3 + (1 - p) * (1 - 2 * h))

    def by_core(zero, one):
        return zero + p * (one - zero)

    class Gather:
        def __init__(self, buf, units, rsem, ssem, nxt, prv, pair):
            self.buf, self.units, self.rsem, self.ssem = buf, units, rsem, ssem
            self.nxt, self.prv, self.pair = nxt, prv, pair

        def plan(self, m):
            nxt, prv, pair = self.nxt, self.prv, self.pair
            ahead = m in FORWARD
            first = [(0, nxt, 1), (0, prv, 2), (0, pair, 3)]
            opposite = (1, nxt, 4) if ahead else (2, prv, 4)
            unit = lambda sends: [(self.units[role], device, there) for role, device, there in sends]
            if m in RELAYED:
                return [unit(sends) for sends in (first, [opposite, (1, pair, 5), (2, pair, 6)], [], [(4, pair, 7)])]
            to_next, to_prev = (3, nxt, 5), (3, prv, 6)
            on, end = (to_next, to_prev) if ahead else (to_prev, to_next)
            last = (5, nxt, 7) if ahead else (6, prv, 7)
            if m != RELAYED_LAST:
                return [unit(sends) for sends in (first, [on], [opposite, end], [last])]
            return [unit(sends) for sends in (first, [on, opposite], [end], [(4, pair, 7)])]

        def sent_on(self, m):
            if m in RELAYED:
                return (4,)
            return (4,) if m == RELAYED_LAST else ((5,) if m in FORWARD else (6,))

        def sends(self, m, level):
            plan = self.plan(m)
            at = sum(len(one) for one in plan[:level])
            made = []
            for index, (unit, device, there) in enumerate(plan[level]):
                place = self.buf.at[unit, part(m)]
                source = xs.at[part(m)] if level == 0 else place
                made.append(copy(source, place, self.ssem.at[m, at + index], self.rsem.at[m, there - 1], device))
            return made

        def arrived(self, m, role):
            place = self.buf.at[self.units[role], part(m)]
            copy(place, place, self.ssem.at[m, 0], self.rsem.at[m, role - 1], self.nxt).wait_recv()

    left = Gather(lf, units_l, r_l, s_l, l_next, l_prev, l_pair)
    right = Gather(rf, units_r, r_r, s_r, r_next, r_prev, r_pair)

    def share(m, role):
        place = rf.at[units_r[role], part(m)]
        return copy(xs.at[part(m)] if role == 0 else place, place, s_r.at[m, 7 + role], r_r.at[m, 7 + role], sibling)

    def shared(m, role):
        place = rf.at[units_s[role], part(m)]
        copy(place, place, s_r.at[m, 0], r_r.at[m, 7 + role], sibling).wait_recv()

    def send_own(m, first=False):
        to_next, to_prev, to_pair = left.sends(m, 0)
        for one in right.sends(m, 0) + [share(m, 0), to_next, to_prev]:
            one.start()
        if first:
            pl.when(jnp.logical_not(moved))(to_pair.start)
        else:
            to_pair.start()

    def split(value):
        top = value.astype(jnp.bfloat16)
        return top, (value - top.astype(jnp.float32)).astype(jnp.bfloat16)

    def keep_left(unit, block, value):
        top, low_part = split(value)
        ls[unit * SLOTS + block, 0:BLK] = top
        ls[unit * SLOTS + block, BLK : 2 * BLK] = low_part

    def keep_right(unit, block, value):
        top, low_part = split(value)
        rs[unit * SLOTS + block, :, 0:BLK] = top
        rs[unit * SLOTS + block, :, BLK : 2 * BLK] = low_part

    def prepare_left(m, role):
        unit = units_l[role]

        @slots(m)
        def _(block):
            keep_left(unit, block, lf[unit, block])

    def prepare_right(m, unit):
        @slots(m)
        def _(block):
            keep_right(unit, block, rf[unit, block])

    diagonal = lax.broadcasted_iota(jnp.int32, (BLK, BLK), 0) == lax.broadcasted_iota(jnp.int32, (BLK, BLK), 1)

    def folded(value):
        return jnp.sum(value.reshape(BLK // 8, 8, BLK), axis=0)

    def total(step, stage):
        def core():
            return copy(sums.at[0], sums.at[1], t_s.at[0, 0], t_r.at[0, 0], sibling)

        def ring(index):
            place, devices = along[index]
            mine = rings.at[index, place]
            return [copy(mine, mine, t_s.at[index + 1, o], t_r.at[index + 1, o], devices[o]) for o in range(3)]

        @pl.when(step == STEPS - 1)
        def _():
            if stage == 0:
                core().start()
                return
            if stage == 1:
                core().wait()
                found = sums[0] + sums[1]
            else:
                for one in ring(stage - 2):
                    one.wait()
                found = (rings[stage - 2, 0] + rings[stage - 2, 1]) + (rings[stage - 2, 2] + rings[stage - 2, 3])
            if stage < 4:
                rings[stage - 1, along[stage - 1][0]] = found
                for one in ring(stage - 1):
                    one.start()
                return
            for at in range(STEPS):
                for which in range(2):
                    place = 2 * at + which
                    traces[which, at] = jnp.sum(found[place : place + 1]) * (1.0 / (ROWS * BR * BLK))

    def lists_copies():
        pairs = (
            (rows_hbm, rows_in),
            (cols_hbm, cols_in),
            (left_hbm, left_in),
            (right_hbm, right_in),
            (target_hbm, target_in),
        )
        for at, (src, dst) in enumerate(pairs):
            yield copy(src, dst, n_s.at[at], n_r.at[at], partner), pltpu.make_async_copy(src, dst, n_r.at[at])

    def build_table():
        for remote, local in lists_copies():
            pl.when(moved)(remote.wait)
            pl.when(jnp.logical_not(moved))(local.wait)
        width = SLOTS * DEPTH
        count = target_in.shape[1]
        lists[...] = jnp.full_like(lists, SLOTS)
        lists[0:1, 0:count] = left_in[...]
        lists[1:2, 0:count] = right_in[...]
        lists[2:3, 0:count] = target_in[...]
        same = (rows_in[...] == cols_in[...]) & (rows_in[...] < ROWS * BR)
        built[2:3, 0:SLOTS] = same.astype(jnp.int32)
        given = lists[...]
        lane = lax.broadcasted_iota(jnp.int32, (BLK, width), 1)
        sublane = lax.broadcasted_iota(jnp.int32, (BLK, width), 0)
        starts_at = range(0, width, BLK)

        def column(row, first):
            one = jnp.transpose(jnp.broadcast_to(row[:, first : first + BLK], (BLK, BLK)))
            return jnp.concatenate([one] * (width // BLK), axis=1)

        rank = jnp.zeros((1, width), jnp.int32)
        for first in starts_at:
            earlier = (column(given[2:3], first) == given[2:3]) & (sublane + first < lane)
            rank += jnp.sum(jnp.where(earlier, 1, 0), axis=0, keepdims=True)
        place = given[2:3] * DEPTH + rank
        lefts = jnp.full((1, width), COLS * SLOTS, jnp.int32)
        rights = jnp.zeros((1, width), jnp.int32)
        for first in starts_at:
            chosen = column(place, first) == lane
            lefts += jnp.sum(jnp.where(chosen, column(given[0:1], first) - COLS * SLOTS, 0), axis=0, keepdims=True)
            rights += jnp.sum(jnp.where(chosen, column(given[1:2], first), 0), axis=0, keepdims=True)
        built[0:1] = lefts
        built[1:2] = rights
        done = pltpu.make_async_copy(built, table, n_r.at[5])
        done.start()
        done.wait()

    def gather(step):
        def send(side, m, number):
            for one in side.sends(m, number):
                one.start()

        def pass_on(m, waits, number):
            for role in waits:
                right.arrived(m, role)
            send(right, m, number)
            for role in waits:
                share(m, role).start()
            for role in waits:
                left.arrived(m, role)
            send(left, m, number)

        def prepare(m, waits):
            for role in waits:
                prepare_left(m, role)
                prepare_right(m, units_r[role])

        def prepare_shared(m, waits):
            for role in waits:
                shared(m, role)
                prepare_right(m, units_s[role])

        for m in range(CHUNKS):
            pass_on(m, (1, 2, 3), 1)
            if m == CHUNKS - 1:
                for after in range(CHUNKS):
                    send(right, after, 2)
                    send(left, after, 2)
            if m == 0:
                pl.when(step == 0)(build_table)
                prepare_own(step)
                total(step, 0)
            prepare(m, (1, 2, 3))
            prepare_shared(m, (0,))
        for m in range(CHUNKS):
            roles_now = left.sent_on(m)
            pass_on(m, roles_now, 3)
            prepare(m, roles_now)
            prepare_shared(m, (1, 2, 3))
        def take(m, waits):
            for role in waits:
                right.arrived(m, role)
                share(m, role).start()
            for role in waits:
                left.arrived(m, role)
            prepare(m, waits)

        for m in range(CHUNKS):
            take(m, [role for role in (4, 5, 6) if role not in left.sent_on(m)])
        for m in range(CHUNKS):
            right.arrived(m, 7)
            share(m, 7).start()
            prepare_right(m, units_r[7])
            prepare_shared(m, (4, 5, 6))
            if m > 0:
                last_share(m - 1)
            if m == CHUNKS - 2:
                pl.when(step < STEPS - 1)(lambda: finish(0))
        for m in range(CHUNKS):
            left.arrived(m, 7)
            prepare_left(m, 7)
        last_share(CHUNKS - 1)

    def last_share(m):
        shared(m, 7)
        prepare_right(m, units_s[7])

    def sent_own(m):
        for one in left.sends(m, 0) + right.sends(m, 0) + [share(m, 0)]:
            one.wait_send()

    def sent_rest(m):
        for number in range(1, 4):
            for one in left.sends(m, number) + right.sends(m, number):
                one.wait_send()
        for role in range(1, 8):
            share(m, role).wait_send()

    def finish(m):
        sent_own(m)
        sent_rest(m)
        for device in neighbours:
            pl.semaphore_signal(credit.at[m], inc=1, device_id=device, device_id_type=MESH)

    def prepare_own(step):
        terms[...] = jnp.zeros_like(terms)

        @pl.loop(0, SLOTS)
        def _(block):
            value = xs[block]
            keep_left(units_l[0], block, value)
            keep_right(units_r[0], block, value)
            weight = table[2, block].astype(jnp.float32)
            terms[0] += folded(jnp.where(diagonal, value, 0.0)) * weight
            terms[1] += folded(value * value)

        for which in range(2):
            sums[0, pl.ds(2 * step + which, 1)] = jnp.sum(terms[which], axis=0, keepdims=True)

    def multiply(step, m):
        @slots(m)
        def _(target):
            lhs = jnp.concatenate([ls[table[0, target * DEPTH + i]] for i in range(DEPTH)], axis=1)
            rhs = jnp.concatenate([rs[table[1, target * DEPTH + i]] for i in range(DEPTH)], axis=0)
            found = jnp.dot(lhs, rhs, preferred_element_type=jnp.float32)
            squared = found[0:BLK, 0:BLK] + (
                found[0:BLK, BLK : 2 * BLK] + found[BLK : 2 * BLK, 0:BLK] + found[BLK : 2 * BLK, BLK : 2 * BLK]
            )
            stored = xs[target]
            taken = (branches[step] == 1).astype(jnp.float32)
            xs[target] = (2.0 - 2.0 * taken) * stored + (2.0 * taken - 1.0) * squared

    def beside(m):
        return copy(x_hbm.at[part(m)], lf.at[units_l[3], part(m)], s_l.at[m, 2], r_l.at[m, 2], sibling)

    for m in range(CHUNKS):
        pl.when(moved)(starts(m).start)
        pl.when(moved)(beside(m).start)
    for remote, local in lists_copies():
        pl.when(moved)(remote.start)
        pl.when(jnp.logical_not(moved))(local.start)
    for m in range(CHUNKS):
        pl.when(moved)(starts(m).wait)
        pl.when(jnp.logical_not(moved))(starts_here(m).wait)
        send_own(m, first=True)

    def finals(m):
        remote = copy(xs.at[part(m)], out_hbm.at[part(m)], fin_s.at[m], fin_r.at[m], partner)
        local = pltpu.make_async_copy(xs.at[part(m)], out_hbm.at[part(m)], fin_r.at[m])
        return remote, local

    @pl.loop(0, STEPS)
    def _(step):
        gather(step)
        total(step, 1)
        for m in range(CHUNKS):
            pl.when(step == STEPS - 1)(lambda m=m: sent_own(m))
            multiply(step, m)

            @pl.when(step < STEPS - 1)
            def _():
                pl.semaphore_wait(credit.at[m], len(neighbours))
                send_own(m)
                if m + 1 < CHUNKS:
                    finish(m + 1)

            @pl.when(step == STEPS - 1)
            def _():
                remote, local = finals(m)
                pl.when(moved)(remote.start)
                pl.when(jnp.logical_not(moved))(local.start)

            if m % 2 == 1:
                total(step, 2 + m // 2)

    for m in range(CHUNKS):
        sent_rest(m)
        remote, local = finals(m)
        pl.when(moved)(remote.wait)
        pl.when(jnp.logical_not(moved))(local.wait)


def run(branches, rows, cols, lefts, rights, targets, blocks):
    dma = pltpu.SemaphoreType.DMA
    main = pl.BlockSpec(memory_space=pltpu.HBM)
    scalars = pl.BlockSpec(memory_space=pltpu.SMEM)
    width = SLOTS * DEPTH
    count = targets.shape[1]
    return pl.pallas_call(
        kernel,
        out_shape=(
            jax.ShapeDtypeStruct((SLOTS, BLK, BLK), jnp.float32),
            jax.ShapeDtypeStruct((2, STEPS), jnp.float32),
        ),
        in_specs=[scalars] + [main] * 6,
        out_specs=(main, scalars),
        scratch_shapes=[
            pltpu.VMEM((SLOTS, BLK, BLK), jnp.float32),
            pltpu.VMEM((COLS, SLOTS, BLK, BLK), jnp.float32),
            pltpu.VMEM((ROWS, SLOTS, BLK, BLK), jnp.float32),
            pltpu.VMEM((COLS * SLOTS + 1, 2 * BLK, BLK), jnp.bfloat16),
            pltpu.VMEM((ROWS * SLOTS, BLK, 2 * BLK), jnp.bfloat16),
            pltpu.VMEM((1, SLOTS), jnp.int32),
            pltpu.VMEM((1, SLOTS), jnp.int32),
            pltpu.VMEM((1, count), jnp.int32),
            pltpu.VMEM((1, count), jnp.int32),
            pltpu.VMEM((1, count), jnp.int32),
            pltpu.VMEM((8, width), jnp.int32),
            pltpu.VMEM((8, width), jnp.int32),
            pltpu.SMEM((8, width), jnp.int32),
            pltpu.VMEM((2, 8, BLK), jnp.float32),
            pltpu.VMEM((2, 8, BLK), jnp.float32),
            pltpu.VMEM((3, 4, 8, BLK), jnp.float32),
            dma((CHUNKS, 7)),
            dma((CHUNKS, 15)),
            dma((CHUNKS, 7)),
            dma((CHUNKS, 15)),
            dma((CHUNKS,)),
            dma((CHUNKS,)),
            dma((CHUNKS,)),
            dma((CHUNKS,)),
            dma((4, 3)),
            dma((4, 3)),
            dma((5,)),
            dma((6,)),
            pltpu.SemaphoreType.REGULAR((CHUNKS,)),
        ],
        compiler_params=pltpu.CompilerParams(
            collective_id=0, has_side_effects=True, vmem_limit_bytes=VMEM_BYTES
        ),
        cost_estimate=pl.CostEstimate(
            flops=STEPS * SLOTS * DEPTH * 8 * BLK**3, bytes_accessed=2 * SLOTS * BLK * BLK * 4, transcendentals=0
        ),
    )(branches, rows, cols, lefts, rights, targets, blocks)


def body(x_tiles, block_rows, block_cols, pair_left, pair_right, pair_target, branches):
    purified, traces = run(
        branches, block_rows[0], block_cols[0], pair_left[0], pair_right[0], pair_target[0], x_tiles[0, 0]
    )
    return (purified[None, None], traces.T)


def solution(mesh):
    placed = (
        P("row", "col", None, None, None),
        P("row", "col", None),
        P("row", "col", None),
        P("row", "col", None),
        P("row", "col", None),
        P("row", "col", None),
        P(),
    )
    return jax.shard_map(
        body,
        mesh=mesh,
        in_specs=placed,
        out_specs=(P("row", "col", None, None, None), P()),
        check_vma=False,
    )
```
